32 devices in a mesh: groups: 2 (over x), row: 16 (over z, y, core).
Axes of the slice: x: 2, y: 2, z: 4, core: 2. Of those that a mesh axis runs over, the one named last changes fastest.
Arguments:
- frames: bfloat16 [6, 64, 128, 16], P('groups', 'row'), parts along dimension 0, may hold values from -6 to 6
- coverage: int32 [64, 256], P('row', 'groups'), parts along dimension 1, may hold values 0 or 1
- h_init: bfloat16 [64, 256, 128], P('row', 'groups'), parts along dimension 1, may hold values from -1 to 1
- c_init: float32 [64, 256, 128], P('row', 'groups'), parts along dimension 1, may hold values from -6 to 6
- m_init: float32 [64, 256, 128], P('row', 'groups'), parts along dimension 1, may hold values from -6 to 6
- w_x: bfloat16 [5, 5, 16, 896], replicated, may hold values from -0.3125 to 0.3125
- w_h: bfloat16 [5, 5, 128, 512], replicated, may hold values from -0.109375 to 0.109375
- w_m: bfloat16 [5, 5, 128, 384], replicated, may hold values from -0.109375 to 0.109375
- w_o: bfloat16 [5, 5, 256, 128], replicated, may hold values from -0.078125 to 0.078125
- w_last: bfloat16 [256, 128], replicated, may hold values from -0.375 to 0.375
- w_out: bfloat16 [128, 16], replicated, may hold values from -0.5 to 0.5
Outputs:
- predicted: bfloat16 [6, 64, 128, 16], P('groups', 'row'), parts along dimension 0
- c_final: float32 [64, 256, 128], P('row', 'groups'), parts along dimension 1
- m_final: float32 [64, 256, 128], P('row', 'groups'), parts along dimension 1
The draws below stay inside these ranges and needn't reach their ends.
There are 2 independent parts, one for each index of `groups`. The reference program is written for one: setup_inputs(seed, part) draws one part's arguments, and reference() takes and returns one part's arrays. A program takes and returns all parts, laid end to end along the dimension named above; an argument that names none is the same for every part. Nothing has to cross between parts.
All inputs are finite; a program needn't handle non-finite values. No bound on the sum of `coverage` on one device may be relied on, other than what follows from the above.
Results may differ from the reference program's by a relative error of at most 0.0061.
Values may be sent and summed in bfloat16 or wider, within the bound.
No kernel may reach another device: no remote copies, remote signals or barrier semaphores. Data moves between devices by JAX's collectives and lax.ppermute only.
A program may use at most 64 MiB of HBM per device.

```python
import jax
import jax.numpy as jnp

CH = 128
CIN = 16
K = 5
STEPS = 3
COLS = 128
NR = 64


def plant(drawn, stream_key, low, largest):
    dims = drawn.shape
    spot = [jax.random.randint(jax.random.fold_in(stream_key, axis), (), 0, dims[axis]) for axis in range(len(dims))]
    drawn = drawn.at[tuple(spot)].set(low)
    longest = dims.index(max(dims))
    spot[longest] = (spot[longest] + 1) % dims[longest]
    return drawn.at[tuple(spot)].set(largest)


def block_levels(stream_key, extent, split, least, largest):
    def one(dim, shards_of):
        heights = jax.random.uniform(jax.random.fold_in(jax.random.fold_in(stream_key, 6), dim), (shards_of,), jnp.float32, least / len(split), largest / len(split))
        return jnp.repeat(jnp.exp(heights), extent[dim] // shards_of).reshape((-1,) + (1,) * (len(extent) - dim - 1))

    factor_of = one(*split[0])
    for cut in split[1:]:
        factor_of = factor_of * one(*cut)
    return factor_of


def gaussian(stream_key, dims, scale, most, shards=(), kind=jnp.bfloat16):
    values = jax.random.normal(stream_key, dims, jnp.float32) * scale
    if len(shards) > 0:
        values = block_levels(stream_key, dims, shards, -0.22, 0.18) * values
    return jnp.clip(values, min=-most, max=most).astype(kind)


def setup_inputs(seed: int = 0, part: int = 0) -> dict:
    seeds = jax.random.split(jax.random.key(seed), 12)
    own_keys = jax.random.split(jax.random.fold_in(seeds[11], part), 12)
    frames = gaussian(own_keys[0], (STEPS, NR, COLS, CIN), 1.0, 6.0, ((1, 16),))
    coverage = plant((jax.random.randint(own_keys[1], (NR, COLS), 0, 8) < 7).astype(jnp.int32), jax.random.fold_in(own_keys[1], 1), 0, 1)
    h_init = jnp.clip(jax.random.uniform(own_keys[2], (NR, COLS, CH), jnp.float32, -1.0, 1.0) * block_levels(own_keys[2], (NR, COLS, CH), ((0, 16),), -0.4, 0.0), -1.0, 1.0).astype(jnp.bfloat16)
    c_init = gaussian(own_keys[3], (NR, COLS, CH), 1.0, 6.0, ((0, 16),), jnp.float32)
    m_init = gaussian(own_keys[4], (NR, COLS, CH), 1.0, 6.0, ((0, 16),), jnp.float32)
    w_x = gaussian(seeds[5], (K, K, CIN, 7 * CH), (K * K * CIN) ** -0.5, 0.3125)
    w_h = gaussian(seeds[6], (K, K, CH, 4 * CH), (K * K * CH) ** -0.5, 0.109375)
    w_m = gaussian(seeds[7], (K, K, CH, 3 * CH), (K * K * CH) ** -0.5, 0.109375)
    w_o = gaussian(seeds[8], (K, K, 2 * CH, CH), (K * K * 2 * CH) ** -0.5, 0.078125)
    w_last = gaussian(seeds[9], (2 * CH, CH), (2 * CH) ** -0.5, 0.375)
    w_out = gaussian(seeds[10], (CH, CIN), CH ** -0.5, 0.5)
    return dict(frames=frames, coverage=coverage, h_init=h_init, c_init=c_init, m_init=m_init, w_x=w_x, w_h=w_h, w_m=w_m, w_o=w_o, w_last=w_last, w_out=w_out)


def convolve(field, weight):
    reach = K // 2
    row_count = field.shape[0]
    col_count = field.shape[1]
    width_in = weight.shape[2]
    padded = jnp.pad(field, ((reach, reach), (reach, reach), (0, 0)))
    summed = jnp.zeros((row_count * col_count, weight.shape[3]), jnp.float32)
    for row_tap in range(K):
        band_rows = padded[row_tap:row_tap + row_count]
        stacked = jnp.concatenate([band_rows[:, col_tap:col_tap + col_count] for col_tap in range(K)], axis=-1)
        summed = summed + jnp.dot(stacked.reshape(-1, K * width_in), weight[row_tap].reshape(K * width_in, -1), preferred_element_type=jnp.float32)
    return summed.reshape(row_count, col_count, -1)


def block_of(values, index, width):
    return values[..., index * width:(index + 1) * width]


def reference(frames, coverage, h_init, c_init, m_init, w_x, w_h, w_m, w_o, w_last, w_out):
    width = CH
    inputs = frames * coverage[None, :, :, None].astype(jnp.bfloat16)
    hidden = h_init
    cell_state = c_init
    memory = m_init
    memory_low = memory.astype(jnp.bfloat16)
    outputs = []
    for moment in range(STEPS):
        from_input = convolve(inputs[moment], w_x)
        from_hidden = convolve(hidden, w_h)
        from_memory = convolve(memory_low, w_m)
        in_gate = jax.nn.sigmoid(block_of(from_input, 0, width) + block_of(from_hidden, 0, width))
        forget = jax.nn.sigmoid(block_of(from_input, 1, width) + block_of(from_hidden, 1, width) + 1.0)
        candidate = jnp.tanh(block_of(from_input, 2, width) + block_of(from_hidden, 2, width))
        cell_state = forget * cell_state + in_gate * candidate
        in_memory = jax.nn.sigmoid(block_of(from_input, 3, width) + block_of(from_memory, 0, width))
        forget_memory = jax.nn.sigmoid(block_of(from_input, 4, width) + block_of(from_memory, 1, width) + 1.0)
        cand_memory = jnp.tanh(block_of(from_input, 5, width) + block_of(from_memory, 2, width))
        memory = forget_memory * memory + in_memory * cand_memory
        memory_low = memory.astype(jnp.bfloat16)
        joined = jnp.concatenate([cell_state.astype(jnp.bfloat16), memory_low], axis=-1)
        out_gate = jax.nn.sigmoid(block_of(from_input, 6, width) + block_of(from_hidden, 3, width) + convolve(joined, w_o))
        mixed = jnp.dot(joined.reshape(-1, 2 * width), w_last, preferred_element_type=jnp.float32).reshape(out_gate.shape)
        hidden = (out_gate * jnp.tanh(mixed)).astype(jnp.bfloat16)
        frame_out = jnp.dot(hidden.reshape(-1, width), w_out, preferred_element_type=jnp.float32).astype(jnp.bfloat16)
        outputs.append(frame_out.reshape(hidden.shape[0], hidden.shape[1], -1))
    return jnp.stack(outputs), cell_state, memory
```

```python
import functools

import jax
import jax.numpy as jnp
from jax import lax
from jax.experimental import pallas as pl
from jax.experimental.pallas import tpu as pltpu
from jax.sharding import PartitionSpec as P

STEPS = 3
TAPS = 5
REACH = 2
LANES = 128
BF = jnp.bfloat16
F32 = jnp.float32


def odd_device():
    return lax.rem(lax.axis_index("row"), 2)


def own_row(e):
    odd = odd_device()
    return e + odd * (3 - 2 * e)


def tap_row(p):
    odd = odd_device()
    return p + odd * (TAPS - 1 - 2 * p)


def sigmoid(x):
    return 0.5 * jnp.tanh(0.5 * x) + 0.5


def clear_pad(pad):
    rows, height = pad.shape[0], pad.shape[1]
    pad[:, :8] = jnp.zeros((rows, 8, LANES), F32)
    pad[:, height - 8 :] = jnp.zeros((rows, 8, LANES), F32)


def put_row(pad, slot, im, row, value, stride, lane0):
    cols = value.shape[0]
    pad[slot, 8 : 8 + cols] = value.astype(F32)
    for s in range(TAPS):
        im[row, :, s * stride + lane0 : s * stride + lane0 + LANES] = pad[
            slot, 6 + s : 6 + s + cols
        ].astype(BF)


def put_frame(pad, slot, im, row, packed, half, moment, width):
    cols = packed.shape[0]
    group = width * (STEPS * half + moment)
    value = packed.astype(F32)
    if group:
        value = pltpu.roll(value, LANES - group, 1)
    lane = lax.broadcasted_iota(jnp.int32, (cols, LANES), 1)
    value = jnp.where(lane < width, value, 0.0)
    pad[slot, 8 : 8 + cols] = value
    total = pad[slot, 6 : 6 + cols]
    for s in range(1, TAPS):
        total = total + pltpu.roll(pad[slot, 6 + s : 6 + s + cols], width * s, 1)
    im[row] = total.astype(BF)


H_PARTS = (
    (0, 256, ((0, 256),), ((0, 256, 0),)),
    (256, 512, ((256, 384), (768, 896)), ((256, 384, 0), (768, 896, 128))),
)
M_PARTS = (
    (0, 256, ((384, 640),), ((384, 640, 0),)),
    (256, 384, ((640, 768),), ((640, 768, 0),)),
)


def add_taps(acc, base, im, im_x, row0, x_row0, weight, w_x, parts, low, high, rows):
    cols = im.shape[1]
    order = range(TAPS) if low == 0 else range(TAPS - 1, -1, -1)
    begun = False
    for p in order:
        r0, r1 = max(0, low - p), min(rows, high - p)
        if r0 >= r1:
            continue
        count = (r1 - r0) * cols
        j = r0 + p
        lhs = jnp.concatenate(
            [
                im[j - row0 : j - row0 + r1 - r0].reshape(count, im.shape[2]),
                im_x[j - x_row0 : j - x_row0 + r1 - r0].reshape(count, LANES),
            ],
            axis=1,
        )
        tap = tap_row(p)
        here = slice(r0 * cols, r1 * cols)
        for c0, c1, x_cols, targets in parts:
            frame = jnp.concatenate([w_x[tap, :, x0:x1] for x0, x1 in x_cols], axis=1)
            fill = jnp.zeros((LANES - w_x.shape[1], c1 - c0), BF)
            rhs = jnp.concatenate([weight[tap, :, c0:c1], frame, fill], axis=0)
            part = jnp.dot(lhs, rhs, preferred_element_type=F32)
            for a0, a1, b0 in targets:
                value = part[:, b0 : b0 + a1 - a0]
                if begun:
                    acc[here, a0:a1] += value
                elif base is None:
                    acc[here, a0:a1] = value
                else:
                    acc[here, a0:a1] = base[here, a0:a1] + value
        begun = True


def new_state(gates, m_gates, width, c_old, m_old):
    def c_gate(k):
        return gates[:, k * width : (k + 1) * width]

    def m_gate(k):
        return m_gates[:, k * width : (k + 1) * width]

    c_new = sigmoid(c_gate(1) + 1.0) * c_old + sigmoid(c_gate(0)) * jnp.tanh(c_gate(2))
    m_new = sigmoid(m_gate(4) + 1.0) * m_old + sigmoid(m_gate(3)) * jnp.tanh(m_gate(5))
    return c_new, m_new


def pack_kernel(h_hbm, c_hbm, m_hbm, f_hbm, cov_hbm, far, near, c_own, m_own, f_ref, cov_ref, sems):
    cols = far.shape[1]
    width = f_ref.shape[2]
    copies = []
    for e in range(4):
        row = own_row(e)
        copies.append((m_hbm.at[row], m_own.at[e]))
        copies.append((c_hbm.at[row], c_own.at[e]))
        copies.append((h_hbm.at[row], far.at[e]))
        if e >= 2:
            copies.append((h_hbm.at[row], near.at[e - 2]))
    copies.append((f_hbm, f_ref))
    copies.append((cov_hbm, cov_ref))
    copies = [pltpu.make_async_copy(a, b, sems.at[i]) for i, (a, b) in enumerate(copies)]
    for copy in copies:
        copy.start()
    for copy in copies:
        copy.wait()
    for e in range(4):
        m = m_own[e].astype(BF)
        far[4 + e] = m
        if e < 2:
            far[8 + e] = c_own[e].astype(BF)
        else:
            near[e] = m
    for unit in range(2):
        parts = []
        for half in range(2):
            row = own_row(2 * unit + half)
            cover = cov_ref[pl.ds(row, 1), :].astype(F32)
            for moment in range(STEPS):
                parts.append(f_ref[moment, row].astype(F32) * cover)
        parts.append(jnp.zeros((LANES - 2 * STEPS * width, cols), F32))
        packed = jnp.concatenate(parts, axis=0).T.astype(BF)
        far[10 + unit] = packed
        if unit == 1:
            near[4] = packed


def local_kernel(moment, width_in, *refs):
    first = moment == 0
    if first:
        (
            far0, near0, c_own, m_own, x_hbm, h_hbm, m_hbm, o_hbm, last_hbm,
            acc, low_ref, c_out, m_out, w_x, w_h, w_m, w_o, w_last,
            pad, im_h, im_m, im_x, sems,
        ) = refs
        copies = [
            pltpu.make_async_copy(a, b, sems.at[i])
            for i, (a, b) in enumerate(
                ((x_hbm, w_x), (h_hbm, w_h), (m_hbm, w_m), (o_hbm, w_o), (last_hbm, w_last))
            )
        ]
        for copy in copies:
            copy.start()
    else:
        (
            far0, near0, arrived0, hid, hid_in, c_edge, m_edge, c_mid, m_mid, low_mid, low_in,
            w_x, w_h, w_m, acc, low_ref, c_out, m_out, im_x, pad, im_h, im_m,
        ) = refs
    cols = far0.shape[1]
    width = far0.shape[2]
    clear_pad(pad)
    for e in range(4):
        put_row(pad, e, im_h, e, far0[e] if first else hid[e], width, 0)
    for k in range(2):
        put_row(pad, 4 + k, im_h, 4 + k, near0[1 - k] if first else hid_in[1 - k], width, 0)
    base = 4 if first else 2
    slot = 16
    for e in range(4):
        put_frame(pad, slot + e, im_x, 4 + e - (4 if first else 0), far0[10 + e // 2], e % 2, moment, width_in)
    for k in range(2):
        put_frame(pad, slot + 4 + k, im_x, 8 + k - (4 if first else 0), near0[4], 1 - k, moment, width_in)
    if not first:
        for k in range(4):
            put_frame(pad, slot + 6 + k, im_x, 3 - k, arrived0[10 + k // 2], k % 2, moment, width_in)
    x_base = 4 if first else 0
    if first:
        for e in range(4):
            put_row(pad, 8 + e, im_m, e, far0[4 + e], width, 0)
        for k in range(2):
            put_row(pad, 12 + k, im_m, 4 + k, near0[3 - k], width, 0)
    else:
        for e in range(4):
            put_row(pad, 8 + e, im_m, e, m_edge[e].astype(BF), width, 0)
        for k in range(2):
            put_row(pad, 12 + k, im_m, 4 + k, low_mid[1, k], width, 0)
            put_row(pad, 14 + k, im_m, 6 + k, low_in[1, 1 - k], width, 0)
    if first:
        copies[0].wait()
        copies[1].wait()
    add_taps(acc, None, im_h, im_x, 4, x_base, w_h, w_x, H_PARTS, 4, 10, 6)
    if first:
        copies[2].wait()
    add_taps(acc, None, im_m, im_x, base, x_base, w_m, w_x, M_PARTS, base, 10, 6)
    for k in range(2):
        c_old, m_old = (c_own[2 + k], m_own[2 + k]) if first else (c_mid[k], m_mid[k])
        gates = acc[(4 + k) * cols : (5 + k) * cols, :]
        c_new, m_new = new_state(gates, gates, width, c_old, m_old)
        c_out[k] = c_new
        m_out[k] = m_new
        low_ref[0, k] = c_new.astype(BF)
        low_ref[1, k] = m_new.astype(BF)
    if first:
        copies[3].wait()
        copies[4].wait()


def final_kernel(moment, last, width_in, *refs):
    first = moment == 0
    refs = list(refs)
    if first:
        arrived, c_edge, m_edge = refs[:3]
        refs = refs[3:]
    else:
        arrived, c_edge, m_edge, im_x = refs[:4]
        refs = refs[4:]
    acc_in, low_mid, low_in, w_x, w_h, w_m, w_o, w_last = refs[:8]
    refs = refs[8:]
    if last:
        hid1, hid2, c_mid, m_mid, w_out, predicted, c_fin, m_fin = refs[:8]
        refs = refs[8:]
    else:
        far, near, c_out, m_out = refs[:4]
        refs = refs[4:]
    pad, im_h, im_m, im_j, acc, gate = refs[:6]
    if first:
        im_x = refs[6]
    if last:
        keep_c, keep_m, sems = refs[6:]
    cols = arrived.shape[1]
    width = arrived.shape[2]
    m_rows = 4 if first else 2
    clear_pad(pad)
    for k in range(4):
        put_row(pad, k, im_h, 3 - k, arrived[k], width, 0)
    for k in range(m_rows):
        put_row(pad, 4 + k, im_m, 3 - k if first else 1 - k, arrived[4 + k], width, 0)
    if first:
        for k in range(4):
            put_frame(pad, 24 + k, im_x, 3 - k, arrived[10 + k // 2], k % 2, moment, width_in)
    for k in range(2):
        for part in range(2):
            put_row(pad, 8 + 2 * k + part, im_j, 4 + k, low_mid[part, k], 2 * width, part * width)
            put_row(pad, 12 + 2 * k + part, im_j, 6 + k, low_in[part, 1 - k], 2 * width, part * width)
    add_taps(acc, acc_in, im_h, im_x, 0, 0, w_h, w_x, H_PARTS, 0, 4, 4)
    add_taps(acc, acc_in, im_m, im_x, 0, 0, w_m, w_x, M_PARTS, 0, m_rows, 4)
    place = lax.axis_index("row")
    inside = jnp.logical_and(place > 0, place < lax.axis_size("row") - 1)
    keep = jnp.where(inside, 1.0, 0.0).astype(F32)
    copies = []
    for r in range(4):
        if first and r < 2:
            c_old, m_old = arrived[9 - r].astype(F32), arrived[5 - r].astype(F32)
        elif first:
            c_old, m_old = c_edge[r - 2], m_edge[r - 2]
        else:
            c_old, m_old = c_edge[r], m_edge[r]
        here = slice(r * cols, (r + 1) * cols)
        gates = acc[here, :]
        m_gates = gates if r < m_rows else acc_in[here, :]
        c_new, m_new = new_state(gates, m_gates, width, c_old, m_old)
        if r < 2:
            c_new, m_new = c_new * keep, m_new * keep
        put_row(pad, 16 + 2 * r, im_j, r, c_new.astype(BF), 2 * width, 0)
        put_row(pad, 17 + 2 * r, im_j, r, m_new.astype(BF), 2 * width, width)
        if not last:
            c_out[r] = c_new
            m_out[r] = m_new
        elif r >= 2:
            keep_c[r - 2] = c_new
            keep_m[r - 2] = m_new
    if last:
        for e in range(4):
            sources = (keep_c.at[e], keep_m.at[e]) if e < 2 else (c_mid.at[e - 2], m_mid.at[e - 2])
            for n, (source, target) in enumerate(zip(sources, (c_fin, m_fin))):
                copies.append(pltpu.make_async_copy(source, target.at[own_row(e)], sems.at[2 * e + n]))
        for copy in copies:
            copy.start()
    for q in range(TAPS + 1):
        lhs = jnp.concatenate([im_j[q], im_j[q + 2]], axis=0)
        if q == 0:
            part = jnp.dot(lhs, w_o[tap_row(0)], preferred_element_type=F32)
            gate[:, :width] = part
        elif q == TAPS:
            part = jnp.dot(lhs, w_o[tap_row(TAPS - 1)], preferred_element_type=F32)
            gate[:, width:] += part
        else:
            rhs = jnp.concatenate([w_o[tap_row(q)], w_o[tap_row(q - 1)]], axis=1)
            part = jnp.dot(lhs, rhs, preferred_element_type=F32)
            gate[:, :width] += part[:, :width]
            if q == 1:
                gate[:, width:] = part[:, width:]
            else:
                gate[:, width:] += part[:, width:]
    rows = []
    for e in range(4):
        joined = im_j[2 + e, :, REACH * 2 * width : (REACH + 1) * 2 * width]
        mixed = jnp.dot(joined, w_last[...], preferred_element_type=F32)
        source = acc if e < 2 else acc_in
        pre = source[(2 + e) * cols : (3 + e) * cols, 6 * width :]
        half = e % 2
        pre = pre + gate[(e // 2) * cols : (e // 2 + 1) * cols, half * width : (half + 1) * width]
        hidden = (sigmoid(pre) * jnp.tanh(mixed)).astype(BF)
        if last:
            rows.append(hidden)
        else:
            far[e] = hidden
            if e >= 2:
                near[e - 2] = hidden
    if not last:
        for k in range(2):
            far[4 + k] = low_mid[1, k]
    else:
        for t, source in enumerate((hid1, hid2, rows)):
            for e in range(4):
                predicted[t, own_row(e)] = lax.dot_general(
                    w_out[...], source[e], (((1,), (1,)), ((), ())), preferred_element_type=F32
                ).astype(BF)
        for copy in copies:
            copy.wait()


VMEM = pl.BlockSpec(memory_space=pltpu.VMEM)
HBM = pl.BlockSpec(memory_space=pltpu.HBM)


def call(body, outs, scratch, args, flops, far_args=(), far_outs=()):
    return pl.pallas_call(
        body,
        out_shape=[jax.ShapeDtypeStruct(shape, kind) for shape, kind in outs],
        in_specs=[HBM if i in far_args else VMEM for i in range(len(args))],
        out_specs=[HBM if i in far_outs else VMEM for i in range(len(outs))],
        scratch_shapes=scratch,
        compiler_params=pltpu.CompilerParams(vmem_limit_bytes=16 * 2**20),
        cost_estimate=pl.CostEstimate(flops=flops, bytes_accessed=4 * 2**20, transcendentals=0),
    )(*args)


def per_device(frames, coverage, h_init, c_init, m_init, w_x, w_h, w_m, w_o, w_last, w_out):
    cols, width = h_init.shape[1], h_init.shape[2]
    width_in = frames.shape[3]
    count = lax.axis_size("row")
    across = [(i, i + 1) for i in range(1, count - 1, 2)]
    across += [(j, i) for i, j in across]
    beside = [(i, i ^ 1) for i in range(count)]
    w_x = w_x.reshape(TAPS, TAPS * width_in, -1)
    w_h = w_h.reshape(TAPS, TAPS * width, -1)
    w_m = w_m.reshape(TAPS, TAPS * width, -1)
    w_o = w_o.reshape(TAPS, TAPS * 2 * width, -1)
    w_out = w_out.T
    gates = w_x.shape[2]

    def rows(n, kind=BF):
        return ((n, cols, width), kind)

    def shaped(w):
        return (w.shape, w.dtype)

    flat = frames.transpose(0, 1, 3, 2)
    h_init, c_init, m_init, flat, coverage, w_x, w_h, w_m, w_o, w_last = (
        pltpu.with_memory_space_constraint(x, pltpu.HBM)
        for x in (h_init, c_init, m_init, flat, coverage, w_x, w_h, w_m, w_o, w_last)
    )
    far0, near0, c_edge, m_edge = call(
        pack_kernel,
        [rows(12), rows(5), rows(4, F32), rows(4, F32)],
        [
            pltpu.VMEM(flat.shape, flat.dtype),
            pltpu.VMEM(coverage.shape, coverage.dtype),
            pltpu.SemaphoreType.DMA((16,)),
        ],
        (h_init, c_init, m_init, flat, coverage),
        10**6,
        far_args=range(5),
    )
    near0_in = lax.ppermute(near0, "row", beside)
    arrived0 = lax.ppermute(far0, "row", across)
    arrived = arrived0
    hiddens = []
    for moment in range(STEPS):
        first, last = moment == 0, moment == STEPS - 1
        outs = [((6 * cols, gates), F32), ((2, 2, cols, width), BF), rows(2, F32), rows(2, F32)]
        scratch = [
            pltpu.VMEM((26, cols + 16, LANES), F32),
            pltpu.VMEM((6, cols, TAPS * width), BF),
            pltpu.VMEM((6 if first else 8, cols, TAPS * width), BF),
        ]
        if first:
            args = (far0, near0_in, c_edge, m_edge, w_x, w_h, w_m, w_o, w_last)
            outs += [shaped(w) for w in args[4:]]
            scratch += [pltpu.VMEM((6, cols, LANES), BF), pltpu.SemaphoreType.DMA((5,))]
            far_args = range(4, 9)
        else:
            args = (far0, near0_in, arrived0, far, near_in, c_edge, m_edge, c_mid, m_mid, low_mid, low_in)
            args += (w_x, w_h, w_m)
            outs.append(((10, cols, LANES), BF))
            far_args = ()
        done = call(
            functools.partial(local_kernel, moment, width_in), outs, scratch, args, 4 * 10**9, far_args
        )
        acc, low_mid, c_mid, m_mid = done[:4]
        if first:
            w_x, w_h, w_m, w_o, w_last = done[4:]
        low_in = lax.ppermute(low_mid, "row", beside)
        args = (arrived, c_edge, m_edge)
        if not first:
            args += (done[4],)
        args += (acc, low_mid, low_in, w_x, w_h, w_m, w_o, w_last)
        far_outs = ()
        if last:
            args += (hiddens[0], hiddens[1], c_mid, m_mid, w_out)
            outs = [((STEPS, 4, width_in, cols), BF), rows(4, F32), rows(4, F32)]
            far_outs = (1, 2)
        else:
            outs = [rows(6), rows(2), rows(4, F32), rows(4, F32)]
        scratch = [
            pltpu.VMEM((32, cols + 16, LANES), F32),
            pltpu.VMEM((4, cols, TAPS * width), BF),
            pltpu.VMEM((4 if first else 2, cols, TAPS * width), BF),
            pltpu.VMEM((8, cols, 2 * TAPS * width), BF),
            pltpu.VMEM((4 * cols, gates), F32),
            pltpu.VMEM((2 * cols, 2 * width), F32),
        ]
        if first:
            scratch.append(pltpu.VMEM((4, cols, LANES), BF))
        if last:
            scratch += [pltpu.VMEM(*rows(2, F32)), pltpu.VMEM(*rows(2, F32)), pltpu.SemaphoreType.DMA((8,))]
        done = call(
            functools.partial(final_kernel, moment, last, width_in),
            outs, scratch, args, 3 * 10**9, far_outs=far_outs,
        )
        if last:
            predicted, c_final, m_final = done
            return predicted.transpose(0, 1, 3, 2), c_final, m_final
        far, near, c_edge, m_edge = done
        hiddens.append(far)
        near_in = lax.ppermute(near, "row", beside)
        arrived = lax.ppermute(far, "row", across)


def solution(mesh):
    placed = (
        P("groups", "row", None, None),
        P("row", "groups"),
        P("row", "groups", None),
        P("row", "groups", None),
        P("row", "groups", None),
        P(),
        P(),
        P(),
        P(),
        P(),
        P(),
    )
    return jax.shard_map(
        per_device,
        mesh=mesh,
        in_specs=placed,
        out_specs=(
            P("groups", "row", None, None),
            P("row", "groups", None),
            P("row", "groups", None),
        ),
        check_vma=False,
    )
```

```python
import functools

import jax
import jax.numpy as jnp
from jax import lax
from jax.experimental import pallas as pl
from jax.experimental.pallas import tpu as pltpu
from jax.sharding import PartitionSpec as P

STEPS = 3
TAPS = 5
REACH = 2
LANES = 128
BF = jnp.bfloat16
F32 = jnp.float32


def odd_device():
    return lax.rem(lax.axis_index("row"), 2)


def own_row(e):
    odd = odd_device()
    return e + odd * (3 - 2 * e)


def tap_row(p):
    odd = odd_device()
    return p + odd * (TAPS - 1 - 2 * p)


def sigmoid(x):
    return 0.5 * jnp.tanh(0.5 * x) + 0.5


def clear_pad(pad):
    rows, height = pad.shape[0], pad.shape[1]
    pad[:, :8] = jnp.zeros((rows, 8, LANES), F32)
    pad[:, height - 8 :] = jnp.zeros((rows, 8, LANES), F32)


def put_row(pad, slot, im, row, value, stride, lane0):
    cols = value.shape[0]
    pad[slot, 8 : 8 + cols] = value.astype(F32)
    for s in range(TAPS):
        im[row, :, s * stride + lane0 : s * stride + lane0 + LANES] = pad[
            slot, 6 + s : 6 + s + cols
        ].astype(BF)


def put_frame(pad, slot, im, row, packed, half, moment, width):
    cols = packed.shape[0]
    group = width * (STEPS * half + moment)
    value = packed.astype(F32)
    if group:
        value = pltpu.roll(value, LANES - group, 1)
    lane = lax.broadcasted_iota(jnp.int32, (cols, LANES), 1)
    value = jnp.where(lane < width, value, 0.0)
    pad[slot, 8 : 8 + cols] = value
    total = pad[slot, 6 : 6 + cols]
    for s in range(1, TAPS):
        total = total + pltpu.roll(pad[slot, 6 + s : 6 + s + cols], width * s, 1)
    im[row] = total.astype(BF)


H_PARTS = (
    (0, 256, ((0, 256),), ((0, 256, 0),)),
    (256, 512, ((256, 384), (768, 896)), ((256, 384, 0), (768, 896, 128))),
)
M_PARTS = (
    (0, 256, ((384, 640),), ((384, 640, 0),)),
    (256, 384, ((640, 768),), ((640, 768, 0),)),
)


def add_taps(acc, base, im, im_x, row0, x_row0, weight, w_x, parts, low, high, rows):
    cols = im.shape[1]
    order = range(TAPS) if low == 0 else range(TAPS - 1, -1, -1)
    begun = False
    for p in order:
        r0, r1 = max(0, low - p), min(rows, high - p)
        if r0 >= r1:
            continue
        count = (r1 - r0) * cols
        j = r0 + p
        lhs = jnp.concatenate(
            [
                im[j - row0 : j - row0 + r1 - r0].reshape(count, im.shape[2]),
                im_x[j - x_row0 : j - x_row0 + r1 - r0].reshape(count, LANES),
            ],
            axis=1,
        )
        tap = tap_row(p)
        here = slice(r0 * cols, r1 * cols)
        for c0, c1, x_cols, targets in parts:
            frame = jnp.concatenate([w_x[tap, :, x0:x1] for x0, x1 in x_cols], axis=1)
            fill = jnp.zeros((LANES - w_x.shape[1], c1 - c0), BF)
            rhs = jnp.concatenate([weight[tap, :, c0:c1], frame, fill], axis=0)
            part = jnp.dot(lhs, rhs, preferred_element_type=F32)
            for a0, a1, b0 in targets:
                value = part[:, b0 : b0 + a1 - a0]
                if begun:
                    acc[here, a0:a1] += value
                elif base is None:
                    acc[here, a0:a1] = value
                else:
                    acc[here, a0:a1] = base[here, a0:a1] + value
        begun = True


def frame_rows(w_x, tap, spans):
    values = jnp.concatenate([w_x[tap, :, a:b] for a, b in spans], axis=1)
    fill = jnp.zeros((LANES - values.shape[0], values.shape[1]), BF)
    return [values, fill]


def add_memory_pairs(acc, im, im_x, row0, x_row0, weight, w_x, low, rows):
    cols = im.shape[1]
    width = weight.shape[2] // 3
    gates = 3 * width

    def lhs_of(j0, j1):
        count = (j1 - j0) * cols
        return jnp.concatenate(
            [
                im[j0 - row0 : j1 - row0].reshape(count, im.shape[2]),
                im_x[j0 - x_row0 : j1 - x_row0].reshape(count, LANES),
            ],
            axis=1,
        )

    def rhs_of(p, a, b):
        tap = tap_row(p)
        rest = frame_rows(w_x, tap, ((gates + a, gates + b),))
        return jnp.concatenate([weight[tap, :, a:b]] + rest, axis=0)

    def product(lhs, rhs):
        return jnp.dot(lhs, rhs, preferred_element_type=F32)

    p = TAPS - 1
    r0 = max(0, low - p)
    lhs = lhs_of(r0 + p, rows + p)
    for a, b in ((0, 2 * width), (2 * width, gates)):
        acc[r0 * cols : rows * cols, gates + a : gates + b] = product(lhs, rhs_of(p, a, b))
    for p in (2, 0):
        q = p + 1
        rp, rq = max(0, low - p), max(0, low - q)
        part = product(lhs_of(rp + p, rows + p), rhs_of(p, 0, 2 * width))
        acc[rp * cols : rows * cols, gates : gates + 2 * width] += part
        part = product(lhs_of(rq + q, rows + q), rhs_of(q, width, gates))
        acc[rq * cols : rows * cols, gates + width : 2 * gates] += part
        j0 = min(rp + p, rq + q)
        rhs = jnp.concatenate([rhs_of(p, 2 * width, gates), rhs_of(q, 0, width)], axis=1)
        part = product(lhs_of(j0, rows + q), rhs)
        a = (rp + p - j0) * cols
        acc[rp * cols : rows * cols, gates + 2 * width : 2 * gates] += part[a : a + (rows - rp) * cols, :width]
        a = (rq + q - j0) * cols
        acc[rq * cols : rows * cols, gates : gates + width] += part[a : a + (rows - rq) * cols, width:]


def new_state(gates, m_gates, width, c_old, m_old):
    def c_gate(k):
        return gates[:, k * width : (k + 1) * width]

    def m_gate(k):
        return m_gates[:, k * width : (k + 1) * width]

    c_new = sigmoid(c_gate(1) + 1.0) * c_old + sigmoid(c_gate(0)) * jnp.tanh(c_gate(2))
    m_new = sigmoid(m_gate(4) + 1.0) * m_old + sigmoid(m_gate(3)) * jnp.tanh(m_gate(5))
    return c_new, m_new


def pack_kernel(h_hbm, c_hbm, m_hbm, f_hbm, cov_hbm, far, near, c_own, m_own, f_ref, cov_ref, sems):
    cols = far.shape[1]
    width = f_ref.shape[2]
    copies = []
    for e in range(4):
        row = own_row(e)
        copies.append((m_hbm.at[row], m_own.at[e]))
        copies.append((c_hbm.at[row], c_own.at[e]))
        copies.append((h_hbm.at[row], far.at[e]))
        if e >= 2:
            copies.append((h_hbm.at[row], near.at[e - 2]))
    copies.append((f_hbm, f_ref))
    copies.append((cov_hbm, cov_ref))
    copies = [pltpu.make_async_copy(a, b, sems.at[i]) for i, (a, b) in enumerate(copies)]
    for copy in copies:
        copy.start()
    for copy in copies:
        copy.wait()
    for e in range(4):
        m = m_own[e].astype(BF)
        far[4 + e] = m
        if e < 2:
            far[8 + e] = c_own[e].astype(BF)
        else:
            near[e] = m
    for unit in range(2):
        parts = []
        for half in range(2):
            row = own_row(2 * unit + half)
            cover = cov_ref[pl.ds(row, 1), :].astype(F32)
            for moment in range(STEPS):
                parts.append(f_ref[moment, row].astype(F32) * cover)
        parts.append(jnp.zeros((LANES - 2 * STEPS * width, cols), F32))
        packed = jnp.concatenate(parts, axis=0).T.astype(BF)
        far[10 + unit] = packed
        if unit == 1:
            near[4] = packed


def local_kernel(moment, width_in, *refs):
    first = moment == 0
    if first:
        (
            far0, near0, c_own, m_own, x_hbm, h_hbm, m_hbm, o_hbm, last_hbm,
            acc, low_ref, c_out, m_out, w_x, w_h, w_m, w_o, w_last,
            pad, im_h, im_m, im_x, sems,
        ) = refs
        copies = [
            pltpu.make_async_copy(a, b, sems.at[i])
            for i, (a, b) in enumerate(
                ((x_hbm, w_x), (h_hbm, w_h), (m_hbm, w_m), (o_hbm, w_o), (last_hbm, w_last))
            )
        ]
        for copy in copies:
            copy.start()
    else:
        (
            far0, near0, arrived0, hid, hid_in, c_edge, m_edge, c_mid, m_mid, low_mid, low_in,
            w_x, w_h, w_m, acc, low_ref, c_out, m_out, im_x, pad, im_h, im_m,
        ) = refs
    cols = far0.shape[1]
    width = far0.shape[2]
    clear_pad(pad)
    for e in range(4):
        put_row(pad, e, im_h, e, far0[e] if first else hid[e], width, 0)
    for k in range(2):
        put_row(pad, 4 + k, im_h, 4 + k, near0[1 - k] if first else hid_in[1 - k], width, 0)
    base = 4 if first else 2
    slot = 16
    for e in range(4):
        put_frame(pad, slot + e, im_x, 4 + e - (4 if first else 0), far0[10 + e // 2], e % 2, moment, width_in)
    for k in range(2):
        put_frame(pad, slot + 4 + k, im_x, 8 + k - (4 if first else 0), near0[4], 1 - k, moment, width_in)
    if not first:
        for k in range(4):
            put_frame(pad, slot + 6 + k, im_x, 3 - k, arrived0[10 + k // 2], k % 2, moment, width_in)
    x_base = 4 if first else 0
    if first:
        for e in range(4):
            put_row(pad, 8 + e, im_m, e, far0[4 + e], width, 0)
        for k in range(2):
            put_row(pad, 12 + k, im_m, 4 + k, near0[3 - k], width, 0)
    else:
        for e in range(4):
            put_row(pad, 8 + e, im_m, e, m_edge[e].astype(BF), width, 0)
        for k in range(2):
            put_row(pad, 12 + k, im_m, 4 + k, low_mid[1, k], width, 0)
            put_row(pad, 14 + k, im_m, 6 + k, low_in[1, 1 - k], width, 0)
    if first:
        copies[0].wait()
        copies[1].wait()
    add_taps(acc, None, im_h, im_x, 4, x_base, w_h, w_x, H_PARTS, 4, 10, 6)
    if first:
        copies[2].wait()
    add_memory_pairs(acc, im_m, im_x, base, x_base, w_m, w_x, base, 6)
    for k in range(2):
        c_old, m_old = (c_own[2 + k], m_own[2 + k]) if first else (c_mid[k], m_mid[k])
        gates = acc[(4 + k) * cols : (5 + k) * cols, :]
        c_new, m_new = new_state(gates, gates, width, c_old, m_old)
        c_out[k] = c_new
        m_out[k] = m_new
        low_ref[0, k] = c_new.astype(BF)
        low_ref[1, k] = m_new.astype(BF)
    if first:
        copies[3].wait()
        copies[4].wait()


def two_taps(lhs, w_o, p, q):
    rhs = jnp.concatenate([w_o[tap_row(p)], w_o[tap_row(q)]], axis=1)
    return jnp.dot(lhs, rhs, preferred_element_type=F32)


def predict(target, hidden, w_out):
    for e in range(4):
        target[e] = lax.dot_general(
            w_out[...], hidden[e], (((1,), (1,)), ((), ())), preferred_element_type=F32
        ).astype(BF)


def inner_kernel(first, *refs):
    if first:
        low_mid, w_o, gate, pad, im = refs
    else:
        low_mid, w_o, hid, w_out, gate, predicted, pad, im = refs
    cols, width = low_mid.shape[2], low_mid.shape[3]
    clear_pad(pad)
    for k in range(2):
        for part in range(2):
            put_row(pad, 2 * k + part, im, k, low_mid[part, k], 2 * width, part * width)
    lhs = im[...].reshape(2 * cols, im.shape[2])
    part = two_taps(lhs, w_o, 4, 3)
    gate[:cols] = part[:cols, :width]
    gate[cols : 2 * cols] = part[cols:, :width] + part[:cols, width:]
    more = two_taps(lhs, w_o, 2, 1)
    gate[2 * cols : 3 * cols] = part[cols:, width:] + more[:cols, :width]
    gate[3 * cols :] = more[cols:, :width] + more[:cols, width:]
    if not first:
        predict(predicted, hid, w_out)


def final_kernel(moment, last, width_in, *refs):
    first = moment == 0
    refs = list(refs)
    if first:
        arrived, c_edge, m_edge = refs[:3]
        refs = refs[3:]
    else:
        arrived, c_edge, m_edge, im_x = refs[:4]
        refs = refs[4:]
    acc_in, low_mid, low_in, gate_in, w_x, w_h, w_m, w_o, w_last = refs[:9]
    refs = refs[9:]
    if last:
        pred1, pred2, c_mid, m_mid, w_out, predicted, c_fin, m_fin = refs[:8]
        refs = refs[8:]
    else:
        far, near, c_out, m_out = refs[:4]
        refs = refs[4:]
    pad, im_h, im_m, im_j, im_i, acc, gate = refs[:7]
    if first:
        im_x = refs[7]
    if last:
        keep_c, keep_m, sems = refs[7:]
    cols = arrived.shape[1]
    width = arrived.shape[2]
    m_rows = 4 if first else 2
    clear_pad(pad)
    for k in range(4):
        put_row(pad, k, im_h, 3 - k, arrived[k], width, 0)
    for k in range(m_rows):
        put_row(pad, 4 + k, im_m, 3 - k if first else 1 - k, arrived[4 + k], width, 0)
    if first:
        for k in range(4):
            put_frame(pad, 24 + k, im_x, 3 - k, arrived[10 + k // 2], k % 2, moment, width_in)
    for k in range(2):
        for part in range(2):
            put_row(pad, 12 + 2 * k + part, im_i, k, low_in[part, 1 - k], 2 * width, part * width)
    add_taps(acc, acc_in, im_h, im_x, 0, 0, w_h, w_x, H_PARTS, 0, 4, 4)
    add_taps(acc, acc_in, im_m, im_x, 0, 0, w_m, w_x, M_PARTS, 0, m_rows, 4)
    place = lax.axis_index("row")
    inside = jnp.logical_and(place > 0, place < lax.axis_size("row") - 1)
    keep = jnp.where(inside, 1.0, 0.0).astype(F32)
    copies = []
    for r in range(4):
        if first and r < 2:
            c_old, m_old = arrived[9 - r].astype(F32), arrived[5 - r].astype(F32)
        elif first:
            c_old, m_old = c_edge[r - 2], m_edge[r - 2]
        else:
            c_old, m_old = c_edge[r], m_edge[r]
        here = slice(r * cols, (r + 1) * cols)
        gates = acc[here, :]
        m_gates = gates if r < m_rows else acc_in[here, :]
        c_new, m_new = new_state(gates, m_gates, width, c_old, m_old)
        if r < 2:
            c_new, m_new = c_new * keep, m_new * keep
        put_row(pad, 16 + 2 * r, im_j, r, c_new.astype(BF), 2 * width, 0)
        put_row(pad, 17 + 2 * r, im_j, r, m_new.astype(BF), 2 * width, width)
        if not last:
            c_out[r] = c_new
            m_out[r] = m_new
        elif r >= 2:
            keep_c[r - 2] = c_new
            keep_m[r - 2] = m_new
    if last:
        for e in range(4):
            sources = (keep_c.at[e], keep_m.at[e]) if e < 2 else (c_mid.at[e - 2], m_mid.at[e - 2])
            for n, (source, target) in enumerate(zip(sources, (c_fin, m_fin))):
                copies.append(pltpu.make_async_copy(source, target.at[own_row(e)], sems.at[2 * e + n]))
        for copy in copies:
            copy.start()
    part = two_taps(im_j[0:4].reshape(4 * cols, -1), w_o, 0, 1)
    gate[...] = part[:, :width] + gate_in[...]
    gate[: 3 * cols] += part[cols:, width:]
    part = two_taps(im_j[2:4].reshape(2 * cols, -1), w_o, 2, 3)
    gate[: 2 * cols] += part[:, :width]
    gate[:cols] += part[cols:, width:]
    part = two_taps(im_i[...].reshape(2 * cols, -1), w_o, 4, 3)
    gate[2 * cols :] += part[:, :width]
    gate[3 * cols :] += part[:cols, width:]
    rows = []
    for e in range(4):
        if e < 2:
            joined = im_j[2 + e, :, REACH * 2 * width : (REACH + 1) * 2 * width]
        else:
            joined = jnp.concatenate([low_mid[0, e - 2], low_mid[1, e - 2]], axis=1)
        mixed = jnp.dot(joined, w_last[...], preferred_element_type=F32)
        source = acc if e < 2 else acc_in
        pre = source[(2 + e) * cols : (3 + e) * cols, 6 * width :]
        pre = pre + gate[e * cols : (e + 1) * cols]
        hidden = (sigmoid(pre) * jnp.tanh(mixed)).astype(BF)
        if last:
            rows.append(hidden)
        else:
            far[e] = hidden
            if e >= 2:
                near[e - 2] = hidden
    if not last:
        for k in range(2):
            far[4 + k] = low_mid[1, k]
    else:
        for e in range(4):
            frame = lax.dot_general(
                w_out[...], rows[e], (((1,), (1,)), ((), ())), preferred_element_type=F32
            )
            for t, value in enumerate((pred1[e], pred2[e], frame.astype(BF))):
                predicted[t, own_row(e)] = value
        for copy in copies:
            copy.wait()


VMEM = pl.BlockSpec(memory_space=pltpu.VMEM)
HBM = pl.BlockSpec(memory_space=pltpu.HBM)


def call(body, outs, scratch, args, flops, far_args=(), far_outs=()):
    return pl.pallas_call(
        body,
        out_shape=[jax.ShapeDtypeStruct(shape, kind) for shape, kind in outs],
        in_specs=[HBM if i in far_args else VMEM for i in range(len(args))],
        out_specs=[HBM if i in far_outs else VMEM for i in range(len(outs))],
        scratch_shapes=scratch,
        compiler_params=pltpu.CompilerParams(vmem_limit_bytes=16 * 2**20),
        cost_estimate=pl.CostEstimate(flops=flops, bytes_accessed=4 * 2**20, transcendentals=0),
    )(*args)


def per_device(frames, coverage, h_init, c_init, m_init, w_x, w_h, w_m, w_o, w_last, w_out):
    cols, width = h_init.shape[1], h_init.shape[2]
    width_in = frames.shape[3]
    count = lax.axis_size("row")
    across = [(i, i + 1) for i in range(1, count - 1, 2)]
    across += [(j, i) for i, j in across]
    beside = [(i, i ^ 1) for i in range(count)]
    w_x = w_x.reshape(TAPS, TAPS * width_in, -1)
    w_h = w_h.reshape(TAPS, TAPS * width, -1)
    w_m = w_m.reshape(TAPS, TAPS * width, -1)
    w_o = w_o.reshape(TAPS, TAPS * 2 * width, -1)
    w_out = w_out.T
    gates = w_x.shape[2]

    def rows(n, kind=BF):
        return ((n, cols, width), kind)

    def shaped(w):
        return (w.shape, w.dtype)

    flat = frames.transpose(0, 1, 3, 2)
    h_init, c_init, m_init, flat, coverage, w_x, w_h, w_m, w_o, w_last = (
        pltpu.with_memory_space_constraint(x, pltpu.HBM)
        for x in (h_init, c_init, m_init, flat, coverage, w_x, w_h, w_m, w_o, w_last)
    )
    far0, near0, c_edge, m_edge = call(
        pack_kernel,
        [rows(12), rows(5), rows(4, F32), rows(4, F32)],
        [
            pltpu.VMEM(flat.shape, flat.dtype),
            pltpu.VMEM(coverage.shape, coverage.dtype),
            pltpu.SemaphoreType.DMA((16,)),
        ],
        (h_init, c_init, m_init, flat, coverage),
        10**6,
        far_args=range(5),
    )
    near0_in = lax.ppermute(near0, "row", beside)
    arrived0 = lax.ppermute(far0, "row", across)
    arrived = arrived0
    frames_out = []
    for moment in range(STEPS):
        first, last = moment == 0, moment == STEPS - 1
        outs = [((6 * cols, gates), F32), ((2, 2, cols, width), BF), rows(2, F32), rows(2, F32)]
        scratch = [
            pltpu.VMEM((26, cols + 16, LANES), F32),
            pltpu.VMEM((6, cols, TAPS * width), BF),
            pltpu.VMEM((6 if first else 8, cols, TAPS * width), BF),
        ]
        if first:
            args = (far0, near0_in, c_edge, m_edge, w_x, w_h, w_m, w_o, w_last)
            outs += [shaped(w) for w in args[4:]]
            scratch += [pltpu.VMEM((6, cols, LANES), BF), pltpu.SemaphoreType.DMA((5,))]
            far_args = range(4, 9)
        else:
            args = (far0, near0_in, arrived0, far, near_in, c_edge, m_edge, c_mid, m_mid, low_mid, low_in)
            args += (w_x, w_h, w_m)
            outs.append(((10, cols, LANES), BF))
            far_args = ()
        done = call(
            functools.partial(local_kernel, moment, width_in), outs, scratch, args, 4 * 10**9, far_args
        )
        acc, low_mid, c_mid, m_mid = done[:4]
        if first:
            w_x, w_h, w_m, w_o, w_last = done[4:]
        low_in = lax.ppermute(low_mid, "row", beside)
        args, outs = (low_mid, w_o), [((4 * cols, width), F32)]
        if not first:
            args += (far, w_out)
            outs.append(((4, width_in, cols), BF))
        scratch = [pltpu.VMEM((4, cols + 16, LANES), F32), pltpu.VMEM((2, cols, 2 * TAPS * width), BF)]
        edge = call(functools.partial(inner_kernel, first), outs, scratch, args, 10**9)
        frames_out += edge[1:]
        args = (arrived, c_edge, m_edge)
        if not first:
            args += (done[4],)
        args += (acc, low_mid, low_in, edge[0], w_x, w_h, w_m, w_o, w_last)
        far_outs = ()
        if last:
            args += (frames_out[0], frames_out[1], c_mid, m_mid, w_out)
            outs = [((STEPS, 4, width_in, cols), BF), rows(4, F32), rows(4, F32)]
            far_outs = (1, 2)
        else:
            outs = [rows(6), rows(2), rows(4, F32), rows(4, F32)]
        scratch = [
            pltpu.VMEM((32, cols + 16, LANES), F32),
            pltpu.VMEM((4, cols, TAPS * width), BF),
            pltpu.VMEM((4 if first else 2, cols, TAPS * width), BF),
            pltpu.VMEM((4, cols, 2 * TAPS * width), BF),
            pltpu.VMEM((2, cols, 2 * TAPS * width), BF),
            pltpu.VMEM((4 * cols, gates), F32),
            pltpu.VMEM((4 * cols, width), F32),
        ]
        if first:
            scratch.append(pltpu.VMEM((4, cols, LANES), BF))
        if last:
            scratch += [pltpu.VMEM(*rows(2, F32)), pltpu.VMEM(*rows(2, F32)), pltpu.SemaphoreType.DMA((8,))]
        done = call(
            functools.partial(final_kernel, moment, last, width_in),
            outs, scratch, args, 3 * 10**9, far_outs=far_outs,
        )
        if last:
            predicted, c_final, m_final = done
            return predicted.transpose(0, 1, 3, 2), c_final, m_final
        far, near, c_edge, m_edge = done
        near_in = lax.ppermute(near, "row", beside)
        arrived = lax.ppermute(far, "row", across)


def solution(mesh):
    placed = (
        P("groups", "row", None, None),
        P("row", "groups"),
        P("row", "groups", None),
        P("row", "groups", None),
        P("row", "groups", None),
        P(),
        P(),
        P(),
        P(),
        P(),
        P(),
    )
    return jax.shard_map(
        per_device,
        mesh=mesh,
        in_specs=placed,
        out_specs=(
            P("groups", "row", None, None),
            P("row", "groups", None),
            P("row", "groups", None),
        ),
        check_vma=False,
    )
```

```python
import functools

import jax
import jax.numpy as jnp
from jax import lax
from jax.experimental import pallas as pl
from jax.experimental.pallas import tpu as pltpu
from jax.sharding import PartitionSpec as P

STEPS = 3
TAPS = 5
REACH = 2
LANES = 128
BF = jnp.bfloat16
F32 = jnp.float32


def odd_device():
    return lax.rem(lax.axis_index("row"), 2)


def own_row(e):
    odd = odd_device()
    return e + odd * (3 - 2 * e)


def tap_row(p):
    odd = odd_device()
    return p + odd * (TAPS - 1 - 2 * p)


def partner_exists():
    place = lax.axis_index("row")
    inside = jnp.logical_and(place > 0, place < lax.axis_size("row") - 1)
    return jnp.where(inside, 1.0, 0.0).astype(F32)


def sigmoid(x):
    return 0.5 * jnp.tanh(0.5 * x) + 0.5


def clear_pad(pad):
    rows, height = pad.shape[0], pad.shape[1]
    pad[:, :8] = jnp.zeros((rows, 8, LANES), F32)
    pad[:, height - 8 :] = jnp.zeros((rows, 8, LANES), F32)


def put_row(pad, slot, im, row, value, stride, lane0):
    cols = value.shape[0]
    pad[slot, 8 : 8 + cols] = value.astype(F32)
    for s in range(TAPS):
        im[row, :, s * stride + lane0 : s * stride + lane0 + LANES] = pad[
            slot, 6 + s : 6 + s + cols
        ].astype(BF)


def put_frame(pad, slot, im, row, packed, half, moment, width):
    cols = packed.shape[0]
    group = width * (STEPS * half + moment)
    value = packed.astype(F32)
    if group:
        value = pltpu.roll(value, LANES - group, 1)
    lane = lax.broadcasted_iota(jnp.int32, (cols, LANES), 1)
    value = jnp.where(lane < width, value, 0.0)
    pad[slot, 8 : 8 + cols] = value
    total = pad[slot, 6 : 6 + cols]
    for s in range(1, TAPS):
        total = total + pltpu.roll(pad[slot, 6 + s : 6 + s + cols], width * s, 1)
    im[row] = total.astype(BF)


H_PARTS = (
    (0, 256, ((0, 256),), ((0, 256, 0),)),
    (256, 512, ((256, 384), (768, 896)), ((256, 384, 0), (768, 896, 128))),
)
M_PARTS = (
    (0, 256, ((384, 640),), ((384, 640, 0),)),
    (256, 384, ((640, 768),), ((640, 768, 0),)),
)


def add_taps(acc, base, im, im_x, row0, x_row0, weight, w_x, parts, low, high, rows):
    cols = im.shape[1]
    order = range(TAPS) if low == 0 else range(TAPS - 1, -1, -1)
    begun = False
    for p in order:
        r0, r1 = max(0, low - p), min(rows, high - p)
        if r0 >= r1:
            continue
        count = (r1 - r0) * cols
        j = r0 + p
        lhs = jnp.concatenate(
            [
                im[j - row0 : j - row0 + r1 - r0].reshape(count, im.shape[2]),
                im_x[j - x_row0 : j - x_row0 + r1 - r0].reshape(count, LANES),
            ],
            axis=1,
        )
        tap = tap_row(p)
        here = slice(r0 * cols, r1 * cols)
        for c0, c1, x_cols, targets in parts:
            frame = jnp.concatenate([w_x[tap, :, x0:x1] for x0, x1 in x_cols], axis=1)
            fill = jnp.zeros((LANES - w_x.shape[1], c1 - c0), BF)
            rhs = jnp.concatenate([weight[tap, :, c0:c1], frame, fill], axis=0)
            part = jnp.dot(lhs, rhs, preferred_element_type=F32)
            for a0, a1, b0 in targets:
                value = part[:, b0 : b0 + a1 - a0]
                if begun:
                    acc[here, a0:a1] += value
                elif base is None:
                    acc[here, a0:a1] = value
                else:
                    acc[here, a0:a1] = base[here, a0:a1] + value
        begun = True


def frame_rows(w_x, tap, spans):
    values = jnp.concatenate([w_x[tap, :, a:b] for a, b in spans], axis=1)
    fill = jnp.zeros((LANES - values.shape[0], values.shape[1]), BF)
    return [values, fill]


def add_memory_pairs(acc, im, im_x, row0, x_row0, weight, w_x, low, rows):
    cols = im.shape[1]
    width = weight.shape[2] // 3
    gates = 3 * width

    def lhs_of(j0, j1):
        count = (j1 - j0) * cols
        return jnp.concatenate(
            [
                im[j0 - row0 : j1 - row0].reshape(count, im.shape[2]),
                im_x[j0 - x_row0 : j1 - x_row0].reshape(count, LANES),
            ],
            axis=1,
        )

    def rhs_of(p, a, b):
        tap = tap_row(p)
        rest = frame_rows(w_x, tap, ((gates + a, gates + b),))
        return jnp.concatenate([weight[tap, :, a:b]] + rest, axis=0)

    def product(lhs, rhs):
        return jnp.dot(lhs, rhs, preferred_element_type=F32)

    p = TAPS - 1
    r0 = max(0, low - p)
    lhs = lhs_of(r0 + p, rows + p)
    for a, b in ((0, 2 * width), (2 * width, gates)):
        acc[r0 * cols : rows * cols, gates + a : gates + b] = product(lhs, rhs_of(p, a, b))
    for p in (2, 0):
        q = p + 1
        rp, rq = max(0, low - p), max(0, low - q)
        part = product(lhs_of(rp + p, rows + p), rhs_of(p, 0, 2 * width))
        acc[rp * cols : rows * cols, gates : gates + 2 * width] += part
        part = product(lhs_of(rq + q, rows + q), rhs_of(q, width, gates))
        acc[rq * cols : rows * cols, gates + width : 2 * gates] += part
        j0 = min(rp + p, rq + q)
        rhs = jnp.concatenate([rhs_of(p, 2 * width, gates), rhs_of(q, 0, width)], axis=1)
        part = product(lhs_of(j0, rows + q), rhs)
        a = (rp + p - j0) * cols
        acc[rp * cols : rows * cols, gates + 2 * width : 2 * gates] += part[a : a + (rows - rp) * cols, :width]
        a = (rq + q - j0) * cols
        acc[rq * cols : rows * cols, gates : gates + width] += part[a : a + (rows - rq) * cols, width:]


def new_state(gates, m_gates, width, c_old, m_old):
    def c_gate(k):
        return gates[:, k * width : (k + 1) * width]

    def m_gate(k):
        return m_gates[:, k * width : (k + 1) * width]

    c_new = sigmoid(c_gate(1) + 1.0) * c_old + sigmoid(c_gate(0)) * jnp.tanh(c_gate(2))
    m_new = sigmoid(m_gate(4) + 1.0) * m_old + sigmoid(m_gate(3)) * jnp.tanh(m_gate(5))
    return c_new, m_new


def pack_kernel(h_hbm, c_hbm, m_hbm, f_hbm, cov_hbm, far, near, c_own, m_own, f_ref, cov_ref, sems):
    cols = far.shape[1]
    width = f_ref.shape[2]
    copies = []
    for e in range(4):
        row = own_row(e)
        copies.append((m_hbm.at[row], m_own.at[e]))
        copies.append((c_hbm.at[row], c_own.at[e]))
        copies.append((h_hbm.at[row], far.at[e]))
        if e >= 2:
            copies.append((h_hbm.at[row], near.at[e - 2]))
    copies.append((f_hbm, f_ref))
    copies.append((cov_hbm, cov_ref))
    copies = [pltpu.make_async_copy(a, b, sems.at[i]) for i, (a, b) in enumerate(copies)]
    for copy in copies:
        copy.start()
    for copy in copies:
        copy.wait()
    for e in range(4):
        m = m_own[e].astype(BF)
        far[4 + e] = m
        if e < 2:
            far[8 + e] = c_own[e].astype(BF)
        else:
            near[e] = m
    for unit in range(2):
        parts = []
        for half in range(2):
            row = own_row(2 * unit + half)
            cover = cov_ref[pl.ds(row, 1), :].astype(F32)
            for moment in range(STEPS):
                parts.append(f_ref[moment, row].astype(F32) * cover)
        parts.append(jnp.zeros((LANES - 2 * STEPS * width, cols), F32))
        packed = jnp.concatenate(parts, axis=0).T.astype(BF)
        far[10 + unit] = packed
        if unit == 1:
            near[4] = packed


def local_kernel(moment, width_in, *refs):
    first = moment == 0
    if first:
        (
            far0, near0, c_own, m_own, x_hbm, h_hbm, m_hbm, o_hbm, last_hbm,
            acc, low_ref, c_out, m_out, w_x, w_h, w_m, w_o, w_last,
            pad, im_h, im_m, im_x, sems,
        ) = refs
        copies = [
            pltpu.make_async_copy(a, b, sems.at[i])
            for i, (a, b) in enumerate(
                ((x_hbm, w_x), (h_hbm, w_h), (m_hbm, w_m), (o_hbm, w_o), (last_hbm, w_last))
            )
        ]
        for copy in copies:
            copy.start()
    else:
        (
            far0, near0, arrived0, hid, hid_in, c_edge, m_edge, c_mid, m_mid, low_mid, low_in,
            w_x, w_h, w_m, acc, low_ref, c_out, m_out, im_x, pad, im_h, im_m,
        ) = refs
    cols = far0.shape[1]
    width = far0.shape[2]
    clear_pad(pad)
    for e in range(4):
        put_row(pad, e, im_h, e, far0[e] if first else hid[e], width, 0)
    for k in range(2):
        put_row(pad, 4 + k, im_h, 4 + k, near0[1 - k] if first else hid_in[1 - k], width, 0)
    base = 4 if first else 2
    slot = 16
    for e in range(4):
        put_frame(pad, slot + e, im_x, 4 + e - (4 if first else 0), far0[10 + e // 2], e % 2, moment, width_in)
    for k in range(2):
        put_frame(pad, slot + 4 + k, im_x, 8 + k - (4 if first else 0), near0[4], 1 - k, moment, width_in)
    if not first:
        keep = partner_exists()
        for k in range(4):
            packed = arrived0[10 + k // 2].astype(F32) * keep
            put_frame(pad, slot + 6 + k, im_x, 3 - k, packed, k % 2, moment, width_in)
    x_base = 4 if first else 0
    if first:
        for e in range(4):
            put_row(pad, 8 + e, im_m, e, far0[4 + e], width, 0)
        for k in range(2):
            put_row(pad, 12 + k, im_m, 4 + k, near0[3 - k], width, 0)
    else:
        for e in range(4):
            put_row(pad, 8 + e, im_m, e, m_edge[e].astype(BF), width, 0)
        for k in range(2):
            put_row(pad, 12 + k, im_m, 4 + k, low_mid[1, k], width, 0)
            put_row(pad, 14 + k, im_m, 6 + k, low_in[1, 1 - k], width, 0)
    if first:
        copies[0].wait()
        copies[1].wait()
    add_taps(acc, None, im_h, im_x, 4, x_base, w_h, w_x, H_PARTS, 4, 10, 6)
    if first:
        copies[2].wait()
    add_memory_pairs(acc, im_m, im_x, base, x_base, w_m, w_x, base, 6)
    for k in range(2):
        c_old, m_old = (c_own[2 + k], m_own[2 + k]) if first else (c_mid[k], m_mid[k])
        gates = acc[(4 + k) * cols : (5 + k) * cols, :]
        c_new, m_new = new_state(gates, gates, width, c_old, m_old)
        c_out[k] = c_new
        m_out[k] = m_new
        low_ref[0, k] = c_new.astype(BF)
        low_ref[1, k] = m_new.astype(BF)
    if first:
        copies[3].wait()
        copies[4].wait()


def two_taps(lhs, w_o, p, q):
    rhs = jnp.concatenate([w_o[tap_row(p)], w_o[tap_row(q)]], axis=1)
    return jnp.dot(lhs, rhs, preferred_element_type=F32)


def predict(target, hidden, w_out):
    for e in range(4):
        target[e] = lax.dot_general(
            w_out[...], hidden[e], (((1,), (1,)), ((), ())), preferred_element_type=F32
        ).astype(BF)


def inner_kernel(first, *refs):
    if first:
        low_mid, w_o, gate, pad, im = refs
    else:
        low_mid, w_o, hid, w_out, gate, predicted, pad, im = refs
    cols, width = low_mid.shape[2], low_mid.shape[3]
    clear_pad(pad)
    for k in range(2):
        for part in range(2):
            put_row(pad, 2 * k + part, im, k, low_mid[part, k], 2 * width, part * width)
    lhs = im[...].reshape(2 * cols, im.shape[2])
    part = two_taps(lhs, w_o, 4, 3)
    gate[:cols] = part[:cols, :width]
    gate[cols : 2 * cols] = part[cols:, :width] + part[:cols, width:]
    more = two_taps(lhs, w_o, 2, 1)
    gate[2 * cols : 3 * cols] = part[cols:, width:] + more[:cols, :width]
    gate[3 * cols :] = more[cols:, :width] + more[:cols, width:]
    if not first:
        predict(predicted, hid, w_out)


def final_kernel(moment, last, width_in, *refs):
    first = moment == 0
    refs = list(refs)
    if first:
        arrived, c_edge, m_edge = refs[:3]
        refs = refs[3:]
    else:
        arrived, c_edge, m_edge, im_x = refs[:4]
        refs = refs[4:]
    acc_in, low_mid, low_in, gate_in, w_x, w_h, w_m, w_o, w_last = refs[:9]
    refs = refs[9:]
    if last:
        pred1, pred2, c_mid, m_mid, w_out, predicted, c_fin, m_fin = refs[:8]
        refs = refs[8:]
    else:
        far, near, c_out, m_out = refs[:4]
        refs = refs[4:]
    pad, im_h, im_m, im_j, im_i, acc, gate = refs[:7]
    if first:
        im_x = refs[7]
    if last:
        keep_c, keep_m, sems = refs[7:]
    cols = arrived.shape[1]
    width = arrived.shape[2]
    m_rows = 4 if first else 2
    clear_pad(pad)
    keep = partner_exists()

    def arrived_row(k):
        return arrived[k].astype(F32) * keep

    for k in range(4):
        put_row(pad, k, im_h, 3 - k, arrived_row(k), width, 0)
    for k in range(m_rows):
        put_row(pad, 4 + k, im_m, 3 - k if first else 1 - k, arrived_row(4 + k), width, 0)
    if first:
        for k in range(4):
            put_frame(pad, 24 + k, im_x, 3 - k, arrived_row(10 + k // 2), k % 2, moment, width_in)
    for k in range(2):
        for part in range(2):
            put_row(pad, 12 + 2 * k + part, im_i, k, low_in[part, 1 - k], 2 * width, part * width)
    add_taps(acc, acc_in, im_h, im_x, 0, 0, w_h, w_x, H_PARTS, 0, 4, 4)
    add_taps(acc, acc_in, im_m, im_x, 0, 0, w_m, w_x, M_PARTS, 0, m_rows, 4)
    copies = []
    for r in range(4):
        if first and r < 2:
            c_old, m_old = arrived[9 - r].astype(F32), arrived[5 - r].astype(F32)
        elif first:
            c_old, m_old = c_edge[r - 2], m_edge[r - 2]
        else:
            c_old, m_old = c_edge[r], m_edge[r]
        here = slice(r * cols, (r + 1) * cols)
        gates = acc[here, :]
        m_gates = gates if r < m_rows else acc_in[here, :]
        c_new, m_new = new_state(gates, m_gates, width, c_old, m_old)
        if r < 2:
            c_new, m_new = c_new * keep, m_new * keep
        put_row(pad, 16 + 2 * r, im_j, r, c_new.astype(BF), 2 * width, 0)
        put_row(pad, 17 + 2 * r, im_j, r, m_new.astype(BF), 2 * width, width)
        if not last:
            c_out[r] = c_new
            m_out[r] = m_new
        elif r >= 2:
            keep_c[r - 2] = c_new
            keep_m[r - 2] = m_new
    if last:
        for e in range(4):
            sources = (keep_c.at[e], keep_m.at[e]) if e < 2 else (c_mid.at[e - 2], m_mid.at[e - 2])
            for n, (source, target) in enumerate(zip(sources, (c_fin, m_fin))):
                copies.append(pltpu.make_async_copy(source, target.at[own_row(e)], sems.at[2 * e + n]))
        for copy in copies:
            copy.start()
    part = two_taps(im_j[0:4].reshape(4 * cols, -1), w_o, 0, 1)
    gate[...] = part[:, :width] + gate_in[...]
    gate[: 3 * cols] += part[cols:, width:]
    part = two_taps(im_j[2:4].reshape(2 * cols, -1), w_o, 2, 3)
    gate[: 2 * cols] += part[:, :width]
    gate[:cols] += part[cols:, width:]
    part = two_taps(im_i[...].reshape(2 * cols, -1), w_o, 4, 3)
    gate[2 * cols :] += part[:, :width]
    gate[3 * cols :] += part[:cols, width:]
    rows = []
    for e in range(4):
        if e < 2:
            joined = im_j[2 + e, :, REACH * 2 * width : (REACH + 1) * 2 * width]
        else:
            joined = jnp.concatenate([low_mid[0, e - 2], low_mid[1, e - 2]], axis=1)
        mixed = jnp.dot(joined, w_last[...], preferred_element_type=F32)
        source = acc if e < 2 else acc_in
        pre = source[(2 + e) * cols : (3 + e) * cols, 6 * width :]
        pre = pre + gate[e * cols : (e + 1) * cols]
        hidden = (sigmoid(pre) * jnp.tanh(mixed)).astype(BF)
        if last:
            rows.append(hidden)
        else:
            far[e] = hidden
            if e >= 2:
                near[e - 2] = hidden
    if not last:
        for k in range(2):
            far[4 + k] = low_mid[1, k]
    else:
        for e in range(4):
            frame = lax.dot_general(
                w_out[...], rows[e], (((1,), (1,)), ((), ())), preferred_element_type=F32
            )
            for t, value in enumerate((pred1[e], pred2[e], frame.astype(BF))):
                predicted[t, own_row(e)] = value
        for copy in copies:
            copy.wait()


VMEM = pl.BlockSpec(memory_space=pltpu.VMEM)
HBM = pl.BlockSpec(memory_space=pltpu.HBM)


def call(body, outs, scratch, args, flops, far_args=(), far_outs=()):
    return pl.pallas_call(
        body,
        out_shape=[jax.ShapeDtypeStruct(shape, kind) for shape, kind in outs],
        in_specs=[HBM if i in far_args else VMEM for i in range(len(args))],
        out_specs=[HBM if i in far_outs else VMEM for i in range(len(outs))],
        scratch_shapes=scratch,
        compiler_params=pltpu.CompilerParams(vmem_limit_bytes=16 * 2**20),
        cost_estimate=pl.CostEstimate(flops=flops, bytes_accessed=4 * 2**20, transcendentals=0),
    )(*args)


def per_device(frames, coverage, h_init, c_init, m_init, w_x, w_h, w_m, w_o, w_last, w_out):
    cols, width = h_init.shape[1], h_init.shape[2]
    width_in = frames.shape[3]
    count = lax.axis_size("row")
    groups = lax.axis_size("groups")
    across = [(g * count + i, g * count + i + 1) for g in range(groups) for i in range(1, count - 1, 2)]
    if groups % 2 == 0:
        across += [(g * count + i, (g + 1) * count + i) for g in range(0, groups, 2) for i in (0, count - 1)]
    across += [(j, i) for i, j in across]
    beside = [(i, i ^ 1) for i in range(count)]
    w_x = w_x.reshape(TAPS, TAPS * width_in, -1)
    w_h = w_h.reshape(TAPS, TAPS * width, -1)
    w_m = w_m.reshape(TAPS, TAPS * width, -1)
    w_o = w_o.reshape(TAPS, TAPS * 2 * width, -1)
    w_out = w_out.T
    gates = w_x.shape[2]

    def rows(n, kind=BF):
        return ((n, cols, width), kind)

    def shaped(w):
        return (w.shape, w.dtype)

    flat = frames.transpose(0, 1, 3, 2)
    h_init, c_init, m_init, flat, coverage, w_x, w_h, w_m, w_o, w_last = (
        pltpu.with_memory_space_constraint(x, pltpu.HBM)
        for x in (h_init, c_init, m_init, flat, coverage, w_x, w_h, w_m, w_o, w_last)
    )
    far0, near0, c_edge, m_edge = call(
        pack_kernel,
        [rows(12), rows(5), rows(4, F32), rows(4, F32)],
        [
            pltpu.VMEM(flat.shape, flat.dtype),
            pltpu.VMEM(coverage.shape, coverage.dtype),
            pltpu.SemaphoreType.DMA((16,)),
        ],
        (h_init, c_init, m_init, flat, coverage),
        10**6,
        far_args=range(5),
    )
    near0_in = lax.ppermute(near0, "row", beside)
    arrived0 = lax.ppermute(far0, ("groups", "row"), across)
    arrived = arrived0
    frames_out = []
    for moment in range(STEPS):
        first, last = moment == 0, moment == STEPS - 1
        outs = [((6 * cols, gates), F32), ((2, 2, cols, width), BF), rows(2, F32), rows(2, F32)]
        scratch = [
            pltpu.VMEM((26, cols + 16, LANES), F32),
            pltpu.VMEM((6, cols, TAPS * width), BF),
            pltpu.VMEM((6 if first else 8, cols, TAPS * width), BF),
        ]
        if first:
            args = (far0, near0_in, c_edge, m_edge, w_x, w_h, w_m, w_o, w_last)
            outs += [shaped(w) for w in args[4:]]
            scratch += [pltpu.VMEM((6, cols, LANES), BF), pltpu.SemaphoreType.DMA((5,))]
            far_args = range(4, 9)
        else:
            args = (far0, near0_in, arrived0, far, near_in, c_edge, m_edge, c_mid, m_mid, low_mid, low_in)
            args += (w_x, w_h, w_m)
            outs.append(((10, cols, LANES), BF))
            far_args = ()
        done = call(
            functools.partial(local_kernel, moment, width_in), outs, scratch, args, 4 * 10**9, far_args
        )
        acc, low_mid, c_mid, m_mid = done[:4]
        if first:
            w_x, w_h, w_m, w_o, w_last = done[4:]
        low_in = lax.ppermute(low_mid, "row", beside)
        args, outs = (low_mid, w_o), [((4 * cols, width), F32)]
        if not first:
            args += (far, w_out)
            outs.append(((4, width_in, cols), BF))
        scratch = [pltpu.VMEM((4, cols + 16, LANES), F32), pltpu.VMEM((2, cols, 2 * TAPS * width), BF)]
        edge = call(functools.partial(inner_kernel, first), outs, scratch, args, 10**9)
        frames_out += edge[1:]
        args = (arrived, c_edge, m_edge)
        if not first:
            args += (done[4],)
        args += (acc, low_mid, low_in, edge[0], w_x, w_h, w_m, w_o, w_last)
        far_outs = ()
        if last:
            args += (frames_out[0], frames_out[1], c_mid, m_mid, w_out)
            outs = [((STEPS, 4, width_in, cols), BF), rows(4, F32), rows(4, F32)]
            far_outs = (1, 2)
        else:
            outs = [rows(6), rows(2), rows(4, F32), rows(4, F32)]
        scratch = [
            pltpu.VMEM((32, cols + 16, LANES), F32),
            pltpu.VMEM((4, cols, TAPS * width), BF),
            pltpu.VMEM((4 if first else 2, cols, TAPS * width), BF),
            pltpu.VMEM((4, cols, 2 * TAPS * width), BF),
            pltpu.VMEM((2, cols, 2 * TAPS * width), BF),
            pltpu.VMEM((4 * cols, gates), F32),
            pltpu.VMEM((4 * cols, width), F32),
        ]
        if first:
            scratch.append(pltpu.VMEM((4, cols, LANES), BF))
        if last:
            scratch += [pltpu.VMEM(*rows(2, F32)), pltpu.VMEM(*rows(2, F32)), pltpu.SemaphoreType.DMA((8,))]
        done = call(
            functools.partial(final_kernel, moment, last, width_in),
            outs, scratch, args, 3 * 10**9, far_outs=far_outs,
        )
        if last:
            predicted, c_final, m_final = done
            return predicted.transpose(0, 1, 3, 2), c_final, m_final
        far, near, c_edge, m_edge = done
        near_in = lax.ppermute(near, "row", beside)
        arrived = lax.ppermute(far, ("groups", "row"), across)


def solution(mesh):
    placed = (
        P("groups", "row", None, None),
        P("row", "groups"),
        P("row", "groups", None),
        P("row", "groups", None),
        P("row", "groups", None),
        P(),
        P(),
        P(),
        P(),
        P(),
        P(),
    )
    return jax.shard_map(
        per_device,
        mesh=mesh,
        in_specs=placed,
        out_specs=(
            P("groups", "row", None, None),
            P("row", "groups", None),
            P("row", "groups", None),
        ),
        check_vma=False,
    )
```

```python
import functools

import jax
import jax.numpy as jnp
from jax import lax
from jax.experimental import pallas as pl
from jax.experimental.pallas import tpu as pltpu
from jax.sharding import PartitionSpec as P

STEPS = 3
TAPS = 5
REACH = 2
LANES = 128
BF = jnp.bfloat16
F32 = jnp.float32


def odd_device():
    return lax.rem(lax.axis_index("row"), 2)


def own_row(e):
    odd = odd_device()
    return e + odd * (3 - 2 * e)


def tap_row(p):
    odd = odd_device()
    return p + odd * (TAPS - 1 - 2 * p)


def partner_exists():
    place = lax.axis_index("row")
    inside = jnp.logical_and(place > 0, place < lax.axis_size("row") - 1)
    return jnp.where(inside, 1.0, 0.0).astype(F32)


def sigmoid(x):
    return 0.5 * jnp.tanh(0.5 * x) + 0.5


def clear_pad(pad):
    rows, height = pad.shape[0], pad.shape[1]
    pad[:, :8] = jnp.zeros((rows, 8, LANES), F32)
    pad[:, height - 8 :] = jnp.zeros((rows, 8, LANES), F32)


def put_row(pad, slot, im, row, value, stride, lane0):
    cols = value.shape[0]
    pad[slot, 8 : 8 + cols] = value.astype(F32)
    for s in range(TAPS):
        im[row, :, s * stride + lane0 : s * stride + lane0 + LANES] = pad[
            slot, 6 + s : 6 + s + cols
        ].astype(BF)


def frame_lane(e, moment, width):
    return width * (2 * e + moment if moment < 2 else e)


def put_frame(pad, slot, im, row, packed, e, moment, width):
    cols = packed.shape[0]
    group = frame_lane(e, moment, width)
    value = packed.astype(F32)
    if group:
        value = pltpu.roll(value, LANES - group, 1)
    lane = lax.broadcasted_iota(jnp.int32, (cols, LANES), 1)
    value = jnp.where(lane < width, value, 0.0)
    pad[slot, 8 : 8 + cols] = value
    total = pad[slot, 6 : 6 + cols]
    for s in range(1, TAPS):
        total = total + pltpu.roll(pad[slot, 6 + s : 6 + s + cols], width * s, 1)
    im[row] = total.astype(BF)


H_PARTS = ((0, 256, ((0, 256),)), (256, 512, ((256, 384), (768, 896))))
M_PARTS = ((0, 256, ((384, 640),)), (256, 384, ((640, 768),)))


def add_last_tap(acc, im, im_x, row0, weight, w_x, parts, rows):
    cols = im.shape[1]
    p = TAPS - 1
    lhs = jnp.concatenate(
        [
            im[p - row0 : p - row0 + rows].reshape(rows * cols, im.shape[2]),
            im_x[p : p + rows].reshape(rows * cols, LANES),
        ],
        axis=1,
    )
    tap = tap_row(p)
    for c0, c1, x_cols in parts:
        rest = frame_rows(w_x, tap, x_cols)
        rhs = jnp.concatenate([weight[tap, :, c0:c1]] + rest, axis=0)
        acc[: rows * cols, c0:c1] += jnp.dot(lhs, rhs, preferred_element_type=F32)


def add_taps(acc, base, im, im_x, row0, x_row0, weight, w_x, parts, low, high, rows):
    cols = im.shape[1]
    order = range(TAPS) if low == 0 else range(TAPS - 1, -1, -1)
    begun = False
    for p in order:
        r0, r1 = max(0, low - p), min(rows, high - p)
        if low and p == TAPS - 1:
            r0 = TAPS - 1
            acc[: r0 * cols, :] = jnp.zeros((r0 * cols, acc.shape[1]), F32)
        if r0 >= r1:
            continue
        count = (r1 - r0) * cols
        j = r0 + p
        lhs = jnp.concatenate(
            [
                im[j - row0 : j - row0 + r1 - r0].reshape(count, im.shape[2]),
                im_x[j - x_row0 : j - x_row0 + r1 - r0].reshape(count, LANES),
            ],
            axis=1,
        )
        tap = tap_row(p)
        here = slice(r0 * cols, r1 * cols)
        for c0, c1, x_cols in parts:
            frame = jnp.concatenate([w_x[tap, :, x0:x1] for x0, x1 in x_cols], axis=1)
            fill = jnp.zeros((LANES - w_x.shape[1], c1 - c0), BF)
            rhs = jnp.concatenate([weight[tap, :, c0:c1], frame, fill], axis=0)
            part = jnp.dot(lhs, rhs, preferred_element_type=F32)
            if begun:
                acc[here, c0:c1] += part
            elif base is None:
                acc[here, c0:c1] = part
            else:
                acc[here, c0:c1] = base[here, c0:c1] + part
        begun = True


def frame_rows(w_x, tap, spans):
    values = jnp.concatenate([w_x[tap, :, a:b] for a, b in spans], axis=1)
    fill = jnp.zeros((LANES - values.shape[0], values.shape[1]), BF)
    return [values, fill]


def add_memory_pairs(acc, im, im_x, row0, x_row0, weight, w_x, low, rows):
    cols = im.shape[1]
    width = weight.shape[2] // 3
    gates = 3 * width

    def lhs_of(j0, j1):
        count = (j1 - j0) * cols
        return jnp.concatenate(
            [
                im[j0 - row0 : j1 - row0].reshape(count, im.shape[2]),
                im_x[j0 - x_row0 : j1 - x_row0].reshape(count, LANES),
            ],
            axis=1,
        )

    def rhs_of(p, a, b):
        tap = tap_row(p)
        rest = frame_rows(w_x, tap, ((gates + a, gates + b),))
        return jnp.concatenate([weight[tap, :, a:b]] + rest, axis=0)

    def product(lhs, rhs):
        return jnp.dot(lhs, rhs, preferred_element_type=F32)

    p = TAPS - 1
    r0 = 4
    acc[: r0 * cols, :] = jnp.zeros((r0 * cols, gates), F32)
    lhs = lhs_of(r0 + p, rows + p)
    for a, b in ((0, 2 * width), (2 * width, gates)):
        acc[r0 * cols : rows * cols, a:b] = product(lhs, rhs_of(p, a, b))
    for p in (2, 0):
        q = p + 1
        rp, rq = max(0, low - p), max(0, low - q)
        part = product(lhs_of(rp + p, rows + p), rhs_of(p, 0, 2 * width))
        acc[rp * cols : rows * cols, : 2 * width] += part
        part = product(lhs_of(rq + q, rows + q), rhs_of(q, width, gates))
        acc[rq * cols : rows * cols, width:gates] += part
        j0 = min(rp + p, rq + q)
        rhs = jnp.concatenate([rhs_of(p, 2 * width, gates), rhs_of(q, 0, width)], axis=1)
        part = product(lhs_of(j0, rows + q), rhs)
        a = (rp + p - j0) * cols
        acc[rp * cols : rows * cols, 2 * width : gates] += part[a : a + (rows - rp) * cols, :width]
        a = (rq + q - j0) * cols
        acc[rq * cols : rows * cols, :width] += part[a : a + (rows - rq) * cols, width:]


def new_state(gates, m_gates, width, c_old, m_old):
    def c_gate(k):
        return gates[:, k * width : (k + 1) * width]

    def m_gate(k):
        return m_gates[:, k * width : (k + 1) * width]

    c_new = sigmoid(c_gate(1) + 1.0) * c_old + sigmoid(c_gate(0)) * jnp.tanh(c_gate(2))
    m_new = sigmoid(m_gate(1) + 1.0) * m_old + sigmoid(m_gate(0)) * jnp.tanh(m_gate(2))
    return c_new, m_new


def pack_kernel(h_hbm, c_hbm, m_hbm, f_hbm, cov_hbm, far, near, c_own, m_own, later, f_ref, cov_ref, sems):
    cols = far.shape[1]
    width = f_ref.shape[2]
    copies = []
    for e in range(4):
        row = own_row(e)
        copies.append((m_hbm.at[row], m_own.at[e]))
        copies.append((c_hbm.at[row], c_own.at[e]))
        copies.append((h_hbm.at[row], far.at[e]))
        if e >= 2:
            copies.append((h_hbm.at[row], near.at[e - 2]))
    copies.append((f_hbm, f_ref))
    copies.append((cov_hbm, cov_ref))
    copies = [pltpu.make_async_copy(a, b, sems.at[i]) for i, (a, b) in enumerate(copies)]
    for copy in copies:
        copy.start()
    for copy in copies:
        copy.wait()
    for e in range(4):
        m = m_own[e].astype(BF)
        far[4 + e] = m
        if e < 2:
            far[8 + e] = c_own[e].astype(BF)
        else:
            near[e] = m
    for unit, moments in enumerate(((0, 1), (2,))):
        parts = []
        for e in range(4):
            row = own_row(e)
            cover = cov_ref[pl.ds(row, 1), :].astype(F32)
            for moment in moments:
                parts.append(f_ref[moment, row].astype(F32) * cover)
        if len(parts) * width < LANES:
            parts.append(jnp.zeros((LANES - len(parts) * width, cols), F32))
        packed = jnp.concatenate(parts, axis=0).T.astype(BF)
        near[4 + unit] = packed
        if unit == 0:
            far[10] = packed
        else:
            later[0] = packed


def memory_kernel(moment, width_in, *refs):
    first = moment == 0
    if first:
        far0, near0, x_hbm, m_hbm, h_hbm, o_hbm, last_hbm, acc, im_x, im, w_x, w_m, w_h, w_o, w_last, pad, sems = refs
        copies = [
            pltpu.make_async_copy(a, b, sems.at[i])
            for i, (a, b) in enumerate(
                ((x_hbm, w_x), (m_hbm, w_m), (h_hbm, w_h), (o_hbm, w_o), (last_hbm, w_last))
            )
        ]
        for copy in copies:
            copy.start()
    else:
        own_x, near0, arrived, m_edge, low_mid, low_in, w_x, w_m, acc, im_x, im, pad = refs
    cols = near0.shape[1]
    width = near0.shape[2]
    clear_pad(pad)
    own_frame = far0[10] if first else own_x[own_x.shape[0] - 1]
    low = 4 if first else 2
    for e in range(4):
        put_row(pad, e, im, e, far0[4 + e] if first else m_edge[e].astype(BF), width, 0)
    for k in range(2):
        if first:
            put_row(pad, 4 + k, im, 4 + k, near0[3 - k], width, 0)
        else:
            put_row(pad, 4 + k, im, 4 + k, low_mid[1, k], width, 0)
            put_row(pad, 6 + k, im, 6 + k, low_in[1, 1 - k], width, 0)
    for e in range(4):
        put_frame(pad, 8 + e, im_x, 4 + e, own_frame, e, moment, width_in)
    for k in range(2):
        put_frame(pad, 12 + k, im_x, 8 + k, near0[4 + moment // 2], 3 - k, moment, width_in)
    if first:
        copies[0].wait()
        copies[1].wait()
    else:
        keep = partner_exists()
        packed = arrived[arrived.shape[0] - 1].astype(F32) * keep
        for k in range(4):
            put_frame(pad, 14 + k, im_x, 3 - k, packed, k, moment, width_in)
    add_memory_pairs(acc, im, im_x, low, 0, w_m, w_x, low, 6)
    if first:
        for copy in copies[2:]:
            copy.wait()


def hidden_kernel(first, *refs):
    hid, hid_in, c_old, m_old, acc_m, im_x, w_x, w_h, acc, low_ref, c_out, m_out, im, pad = refs
    cols = hid.shape[1]
    width = hid.shape[2]
    clear_pad(pad)
    for e in range(4):
        put_row(pad, e, im, e, hid[e], width, 0)
    for k in range(2):
        put_row(pad, 4 + k, im, 4 + k, hid_in[1 - k], width, 0)
    add_taps(acc, None, im, im_x, 4, 0, w_h, w_x, H_PARTS, 4, 10, 6)
    for k in range(2):
        here = slice((4 + k) * cols, (5 + k) * cols)
        old = 2 + k if first else k
        c_new, m_new = new_state(acc[here, :], acc_m[here, :], width, c_old[old], m_old[old])
        c_out[k] = c_new
        m_out[k] = m_new
        low_ref[0, k] = c_new.astype(BF)
        low_ref[1, k] = m_new.astype(BF)


def two_taps(lhs, w_o, p, q):
    rhs = jnp.concatenate([w_o[tap_row(p)], w_o[tap_row(q)]], axis=1)
    return jnp.dot(lhs, rhs, preferred_element_type=F32)


def predict(target, hidden, w_out):
    for e in range(4):
        target[e] = lax.dot_general(
            w_out[...], hidden[e], (((1,), (1,)), ((), ())), preferred_element_type=F32
        ).astype(BF)


def inner_kernel(first, *refs):
    acc_old, acc_m_old, im_h, im_m, im_x, w_x, w_h, w_m, low_mid, w_o = refs[:10]
    if first:
        acc, acc_m, gate, pad, im = refs[10:]
    else:
        hid, w_out, acc, acc_m, gate, predicted, pad, im = refs[10:]
    cols, width = low_mid.shape[2], low_mid.shape[3]
    clear_pad(pad)
    for k in range(2):
        for part in range(2):
            put_row(pad, 2 * k + part, im, k, low_mid[part, k], 2 * width, part * width)
    lhs = im[...].reshape(2 * cols, im.shape[2])
    part = two_taps(lhs, w_o, 4, 3)
    gate[:cols] = part[:cols, :width]
    gate[cols : 2 * cols] = part[cols:, :width] + part[:cols, width:]
    more = two_taps(lhs, w_o, 2, 1)
    gate[2 * cols : 3 * cols] = part[cols:, width:] + more[:cols, :width]
    gate[3 * cols :] = more[cols:, :width] + more[:cols, width:]
    add_last_tap(acc, im_h, im_x, 4, w_h, w_x, H_PARTS, 4)
    add_last_tap(acc_m, im_m, im_x, 4 if first else 2, w_m, w_x, M_PARTS, 4)
    if not first:
        predict(predicted, hid, w_out)


def final_kernel(moment, last, width_in, *refs):
    first = moment == 0
    refs = list(refs)
    if first:
        arrived, c_edge, m_edge, later = refs[:4]
        refs = refs[4:]
    else:
        arrived, c_edge, m_edge, im_x = refs[:4]
        refs = refs[4:]
    acc_in, acc_m_in, low_mid, low_in, gate_in, w_x, w_h, w_m, w_o, w_last = refs[:10]
    refs = refs[10:]
    if last:
        pred1, pred2, c_mid, m_mid, w_out, predicted, c_fin, m_fin = refs[:8]
        refs = refs[8:]
    else:
        far, near, c_out, m_out = refs[:4]
        refs = refs[4:]
    pad, im_h, im_m, im_j, im_i, acc, acc_m, gate = refs[:8]
    if first:
        im_x = refs[8]
    if last:
        keep_c, keep_m, frame, sems = refs[8:]
    cols = arrived.shape[1]
    width = arrived.shape[2]
    m_rows = 4 if first else 2
    clear_pad(pad)
    keep = partner_exists()

    def arrived_row(k):
        return arrived[k].astype(F32) * keep

    for k in range(4):
        put_row(pad, k, im_h, 3 - k, arrived_row(k), width, 0)
    for k in range(m_rows):
        put_row(pad, 4 + k, im_m, 3 - k if first else 1 - k, arrived_row(4 + k), width, 0)
    if first:
        for k in range(4):
            put_frame(pad, 24 + k, im_x, 3 - k, arrived_row(10), k, moment, width_in)
    for k in range(2):
        for part in range(2):
            put_row(pad, 12 + 2 * k + part, im_i, k, low_in[part, 1 - k], 2 * width, part * width)
    add_taps(acc, acc_in, im_h, im_x, 0, 0, w_h, w_x, H_PARTS, 0, 4, 4)
    add_taps(acc_m, acc_m_in, im_m, im_x, 0, 0, w_m, w_x, M_PARTS, 0, m_rows, 4)
    copies = []
    for r in range(4):
        if first and r < 2:
            c_old, m_old = arrived[9 - r].astype(F32), arrived[5 - r].astype(F32)
        elif first:
            c_old, m_old = c_edge[r - 2], m_edge[r - 2]
        else:
            c_old, m_old = c_edge[r], m_edge[r]
        here = slice(r * cols, (r + 1) * cols)
        gates = acc[here, :]
        m_gates = (acc_m if r < m_rows else acc_m_in)[here, :]
        c_new, m_new = new_state(gates, m_gates, width, c_old, m_old)
        if r < 2:
            c_new, m_new = c_new * keep, m_new * keep
        put_row(pad, 16 + 2 * r, im_j, r, c_new.astype(BF), 2 * width, 0)
        put_row(pad, 17 + 2 * r, im_j, r, m_new.astype(BF), 2 * width, width)
        if not last:
            c_out[r] = c_new
            m_out[r] = m_new
        elif r >= 2:
            keep_c[r - 2] = c_new
            keep_m[r - 2] = m_new
    if last:
        for e in range(4):
            sources = (keep_c.at[e], keep_m.at[e]) if e < 2 else (c_mid.at[e - 2], m_mid.at[e - 2])
            for n, (source, target) in enumerate(zip(sources, (c_fin, m_fin))):
                copies.append(pltpu.make_async_copy(source, target.at[own_row(e)], sems.at[2 * e + n]))
            for t, source in enumerate((pred1, pred2)):
                target = predicted.at[t, own_row(e)]
                copies.append(pltpu.make_async_copy(source.at[e], target, sems.at[8 + 2 * e + t]))
        for copy in copies:
            copy.start()
    part = two_taps(im_j[0:4].reshape(4 * cols, -1), w_o, 0, 1)
    gate[...] = part[:, :width] + gate_in[...]
    gate[: 3 * cols] += part[cols:, width:]
    part = two_taps(im_j[2:4].reshape(2 * cols, -1), w_o, 2, 3)
    gate[: 2 * cols] += part[:, :width]
    gate[:cols] += part[cols:, width:]
    part = two_taps(im_i[...].reshape(2 * cols, -1), w_o, 4, 3)
    gate[2 * cols :] += part[:, :width]
    gate[3 * cols :] += part[:cols, width:]
    rows = []
    for e in range(4):
        if e < 2:
            joined = im_j[2 + e, :, REACH * 2 * width : (REACH + 1) * 2 * width]
        else:
            joined = jnp.concatenate([low_mid[0, e - 2], low_mid[1, e - 2]], axis=1)
        mixed = jnp.dot(joined, w_last[...], preferred_element_type=F32)
        source = acc if e < 2 else acc_in
        pre = source[(2 + e) * cols : (3 + e) * cols, 3 * width :]
        pre = pre + gate[e * cols : (e + 1) * cols]
        hidden = (sigmoid(pre) * jnp.tanh(mixed)).astype(BF)
        if last:
            rows.append(hidden)
        else:
            far[e] = hidden
            if e >= 2:
                near[e - 2] = hidden
    if not last:
        for k in range(2):
            far[4 + k] = low_mid[1, k]
        if first:
            far[6] = later[0]
    else:
        for e in range(4):
            frame[e] = lax.dot_general(
                w_out[...], rows[e], (((1,), (1,)), ((), ())), preferred_element_type=F32
            ).astype(BF)
            copies.append(pltpu.make_async_copy(frame.at[e], predicted.at[2, own_row(e)], sems.at[16 + e]))
            copies[-1].start()
        for copy in copies:
            copy.wait()


VMEM = pl.BlockSpec(memory_space=pltpu.VMEM)
HBM = pl.BlockSpec(memory_space=pltpu.HBM)


def call(body, outs, scratch, args, flops, far_args=(), far_outs=(), aliases=None):
    return pl.pallas_call(
        body,
        out_shape=[jax.ShapeDtypeStruct(shape, kind) for shape, kind in outs],
        in_specs=[HBM if i in far_args else VMEM for i in range(len(args))],
        out_specs=[HBM if i in far_outs else VMEM for i in range(len(outs))],
        scratch_shapes=scratch,
        input_output_aliases=aliases or {},
        compiler_params=pltpu.CompilerParams(vmem_limit_bytes=16 * 2**20),
        cost_estimate=pl.CostEstimate(flops=flops, bytes_accessed=4 * 2**20, transcendentals=0),
    )(*args)


def per_device(frames, coverage, h_init, c_init, m_init, w_x, w_h, w_m, w_o, w_last, w_out):
    cols, width = h_init.shape[1], h_init.shape[2]
    width_in = frames.shape[3]
    count = lax.axis_size("row")
    groups = lax.axis_size("groups")
    across = [(g * count + i, g * count + i + 1) for g in range(groups) for i in range(1, count - 1, 2)]
    if groups % 2 == 0:
        across += [(g * count + i, (g + 1) * count + i) for g in range(0, groups, 2) for i in (0, count - 1)]
    across += [(j, i) for i, j in across]
    beside = [(i, i ^ 1) for i in range(count)]
    w_x = w_x.reshape(TAPS, TAPS * width_in, -1)
    w_h = w_h.reshape(TAPS, TAPS * width, -1)
    w_m = w_m.reshape(TAPS, TAPS * width, -1)
    w_o = w_o.reshape(TAPS, TAPS * 2 * width, -1)
    w_out = w_out.T

    def rows(n, kind=BF):
        return ((n, cols, width), kind)

    def shaped(w):
        return (w.shape, w.dtype)

    flat = frames.transpose(0, 1, 3, 2)
    h_init, c_init, m_init, flat, coverage, w_x, w_h, w_m, w_o, w_last = (
        pltpu.with_memory_space_constraint(x, pltpu.HBM)
        for x in (h_init, c_init, m_init, flat, coverage, w_x, w_h, w_m, w_o, w_last)
    )
    far0, near0, c_edge, m_edge, later = call(
        pack_kernel,
        [rows(11), rows(6), rows(4, F32), rows(4, F32), rows(1)],
        [
            pltpu.VMEM(flat.shape, flat.dtype),
            pltpu.VMEM(coverage.shape, coverage.dtype),
            pltpu.SemaphoreType.DMA((16,)),
        ],
        (h_init, c_init, m_init, flat, coverage),
        10**6,
        far_args=range(5),
    )
    near0_in = lax.ppermute(near0, "row", beside)
    arrived = lax.ppermute(far0, ("groups", "row"), across)
    frames_out = []
    for moment in range(STEPS):
        first, last = moment == 0, moment == STEPS - 1
        outs = [
            ((6 * cols, 3 * width), F32),
            ((10, cols, LANES), BF),
            ((6 if first else 8, cols, TAPS * width), BF),
        ]
        scratch = [pltpu.VMEM((18, cols + 16, LANES), F32)]
        if first:
            args = (far0, near0_in, w_x, w_m, w_h, w_o, w_last)
            outs += [shaped(w) for w in args[2:]]
            scratch.append(pltpu.SemaphoreType.DMA((5,)))
            far_args = range(2, 7)
        else:
            args = (later if last else far0, near0_in, frames_in, m_edge, low_mid, low_in, w_x, w_m)
            far_args = ()
        done = call(
            functools.partial(memory_kernel, moment, width_in), outs, scratch, args, 2 * 10**9, far_args
        )
        acc_m, im_x, im_m = done[:3]
        if first:
            w_x, w_m, w_h, w_o, w_last = done[3:]
            args = (far0, near0_in, c_edge, m_edge)
        else:
            args = (far, near_in, c_mid, m_mid)
        outs = [((6 * cols, 4 * width), F32), ((2, 2, cols, width), BF), rows(2, F32), rows(2, F32)]
        outs.append(((6, cols, TAPS * width), BF))
        scratch = [pltpu.VMEM((6, cols + 16, LANES), F32)]
        acc, low_mid, c_mid, m_mid, im_h = call(
            functools.partial(hidden_kernel, first), outs, scratch, args + (acc_m, im_x, w_x, w_h), 2 * 10**9
        )
        low_in = lax.ppermute(low_mid, "row", beside)
        args = (acc, acc_m, im_h, im_m, im_x, w_x, w_h, w_m, low_mid, w_o)
        outs = [((6 * cols, 4 * width), F32), ((6 * cols, 3 * width), F32), ((4 * cols, width), F32)]
        if not first:
            args += (far, w_out)
            outs.append(((4, width_in, cols), BF))
        scratch = [pltpu.VMEM((4, cols + 16, LANES), F32), pltpu.VMEM((2, cols, 2 * TAPS * width), BF)]
        edge = call(functools.partial(inner_kernel, first), outs, scratch, args, 10**9, aliases={0: 0, 1: 1})
        acc, acc_m = edge[:2]
        frames_out += edge[3:]
        frames_in = arrived
        args = (arrived, c_edge, m_edge)
        if first:
            args += (later,)
        if not first:
            args += (im_x,)
        args += (acc, acc_m, low_mid, low_in, edge[2], w_x, w_h, w_m, w_o, w_last)
        far_outs = ()
        if last:
            args += (frames_out[0], frames_out[1], c_mid, m_mid, w_out)
            outs = [((STEPS, 4, width_in, cols), BF), rows(4, F32), rows(4, F32)]
            far_outs = (0, 1, 2)
        else:
            outs = [rows(7 if first else 6), rows(2), rows(4, F32), rows(4, F32)]
        scratch = [
            pltpu.VMEM((32, cols + 16, LANES), F32),
            pltpu.VMEM((4, cols, TAPS * width), BF),
            pltpu.VMEM((4 if first else 2, cols, TAPS * width), BF),
            pltpu.VMEM((4, cols, 2 * TAPS * width), BF),
            pltpu.VMEM((2, cols, 2 * TAPS * width), BF),
            pltpu.VMEM((4 * cols, 4 * width), F32),
            pltpu.VMEM((4 * cols, 3 * width), F32),
            pltpu.VMEM((4 * cols, width), F32),
        ]
        if first:
            scratch.append(pltpu.VMEM((4, cols, LANES), BF))
        if last:
            scratch += [
                pltpu.VMEM(*rows(2, F32)),
                pltpu.VMEM(*rows(2, F32)),
                pltpu.VMEM((4, width_in, cols), BF),
                pltpu.SemaphoreType.DMA((20,)),
            ]
        done = call(
            functools.partial(final_kernel, moment, last, width_in),
            outs, scratch, args, 3 * 10**9, far_outs=far_outs,
        )
        if last:
            predicted, c_final, m_final = done
            return predicted.transpose(0, 1, 3, 2), c_final, m_final
        far, near, c_edge, m_edge = done
        near_in = lax.ppermute(near, "row", beside)
        arrived = lax.ppermute(far, ("groups", "row"), across)


def solution(mesh):
    placed = (
        P("groups", "row", None, None),
        P("row", "groups"),
        P("row", "groups", None),
        P("row", "groups", None),
        P("row", "groups", None),
        P(),
        P(),
        P(),
        P(),
        P(),
        P(),
    )
    return jax.shard_map(
        per_device,
        mesh=mesh,
        in_specs=placed,
        out_specs=(
            P("groups", "row", None, None),
            P("row", "groups", None),
            P("row", "groups", None),
        ),
        check_vma=False,
    )
```

```python
import functools

import jax
import jax.numpy as jnp
from jax import lax
from jax.experimental import pallas as pl
from jax.experimental.pallas import tpu as pltpu
from jax.sharding import PartitionSpec as P

STEPS = 3
TAPS = 5
REACH = 2
LANES = 128
BF = jnp.bfloat16
F32 = jnp.float32


def odd_device():
    return lax.rem(lax.axis_index("row"), 2)


def own_row(e):
    odd = odd_device()
    return e + odd * (3 - 2 * e)


def tap_row(p):
    odd = odd_device()
    return p + odd * (TAPS - 1 - 2 * p)


def partner_exists():
    place = lax.axis_index("row")
    inside = jnp.logical_and(place > 0, place < lax.axis_size("row") - 1)
    return jnp.where(inside, 1.0, 0.0).astype(F32)


def sigmoid(x):
    return 0.5 * jnp.tanh(0.5 * x) + 0.5


def clear_pad(pad):
    rows, height = pad.shape[0], pad.shape[1]
    pad[:, :8] = jnp.zeros((rows, 8, LANES), F32)
    pad[:, height - 8 :] = jnp.zeros((rows, 8, LANES), F32)


def put_row(pad, slot, im, row, value, stride, lane0):
    cols = value.shape[0]
    pad[slot, 8 : 8 + cols] = value.astype(F32)
    for s in range(TAPS):
        im[row, :, s * stride + lane0 : s * stride + lane0 + LANES] = pad[
            slot, 6 + s : 6 + s + cols
        ].astype(BF)


def frame_lane(e, moment, width):
    return width * (2 * e + moment if moment < 2 else e)


def put_frame(pad, slot, im, row, packed, e, moment, width):
    cols = packed.shape[0]
    group = frame_lane(e, moment, width)
    value = packed.astype(F32)
    if group:
        value = pltpu.roll(value, LANES - group, 1)
    lane = lax.broadcasted_iota(jnp.int32, (cols, LANES), 1)
    value = jnp.where(lane < width, value, 0.0)
    pad[slot, 8 : 8 + cols] = value
    total = pad[slot, 6 : 6 + cols]
    for s in range(1, TAPS):
        total = total + pltpu.roll(pad[slot, 6 + s : 6 + s + cols], width * s, 1)
    im[row] = total.astype(BF)


H_PARTS = ((0, 256, ((0, 256),)), (256, 512, ((256, 384), (768, 896))))
M_PARTS = ((0, 256, ((384, 640),)), (256, 384, ((640, 768),)))


def add_last_tap(acc, im, im_x, row0, weight, w_x, parts, rows):
    cols = im.shape[1]
    p = TAPS - 1
    lhs = jnp.concatenate(
        [
            im[p - row0 : p - row0 + rows].reshape(rows * cols, im.shape[2]),
            im_x[p : p + rows].reshape(rows * cols, LANES),
        ],
        axis=1,
    )
    tap = tap_row(p)
    for c0, c1, x_cols in parts:
        rest = frame_rows(w_x, tap, x_cols)
        rhs = jnp.concatenate([weight[tap, :, c0:c1]] + rest, axis=0)
        acc[: rows * cols, c0:c1] += jnp.dot(lhs, rhs, preferred_element_type=F32)


def add_taps(acc, base, im, im_x, row0, x_row0, weight, w_x, parts, low, high, rows):
    cols = im.shape[1]
    order = range(TAPS) if low == 0 else range(TAPS - 1, -1, -1)
    begun = False
    for p in order:
        r0, r1 = max(0, low - p), min(rows, high - p)
        if low and p == TAPS - 1:
            r0 = TAPS - 1
            acc[: r0 * cols, :] = jnp.zeros((r0 * cols, acc.shape[1]), F32)
        if r0 >= r1:
            continue
        count = (r1 - r0) * cols
        j = r0 + p
        lhs = jnp.concatenate(
            [
                im[j - row0 : j - row0 + r1 - r0].reshape(count, im.shape[2]),
                im_x[j - x_row0 : j - x_row0 + r1 - r0].reshape(count, LANES),
            ],
            axis=1,
        )
        tap = tap_row(p)
        here = slice(r0 * cols, r1 * cols)
        for c0, c1, x_cols in parts:
            frame = jnp.concatenate([w_x[tap, :, x0:x1] for x0, x1 in x_cols], axis=1)
            fill = jnp.zeros((LANES - w_x.shape[1], c1 - c0), BF)
            rhs = jnp.concatenate([weight[tap, :, c0:c1], frame, fill], axis=0)
            part = jnp.dot(lhs, rhs, preferred_element_type=F32)
            if begun:
                acc[here, c0:c1] += part
            elif base is None:
                acc[here, c0:c1] = part
            else:
                acc[here, c0:c1] = base[here, c0:c1] + part
        begun = True


def frame_rows(w_x, tap, spans):
    values = jnp.concatenate([w_x[tap, :, a:b] for a, b in spans], axis=1)
    fill = jnp.zeros((LANES - values.shape[0], values.shape[1]), BF)
    return [values, fill]


def add_memory_pairs(acc, im, im_x, row0, x_row0, weight, w_x, low, rows):
    cols = im.shape[1]
    width = weight.shape[2] // 3
    gates = 3 * width

    def lhs_of(j0, j1):
        count = (j1 - j0) * cols
        return jnp.concatenate(
            [
                im[j0 - row0 : j1 - row0].reshape(count, im.shape[2]),
                im_x[j0 - x_row0 : j1 - x_row0].reshape(count, LANES),
            ],
            axis=1,
        )

    def rhs_of(p, a, b):
        tap = tap_row(p)
        rest = frame_rows(w_x, tap, ((gates + a, gates + b),))
        return jnp.concatenate([weight[tap, :, a:b]] + rest, axis=0)

    def product(lhs, rhs):
        return jnp.dot(lhs, rhs, preferred_element_type=F32)

    p = TAPS - 1
    r0 = 4
    acc[: r0 * cols, :] = jnp.zeros((r0 * cols, gates), F32)
    lhs = lhs_of(r0 + p, rows + p)
    for a, b in ((0, 2 * width), (2 * width, gates)):
        acc[r0 * cols : rows * cols, a:b] = product(lhs, rhs_of(p, a, b))
    for p in (2, 0):
        q = p + 1
        rp, rq = max(0, low - p), max(0, low - q)
        part = product(lhs_of(rp + p, rows + p), rhs_of(p, 0, 2 * width))
        acc[rp * cols : rows * cols, : 2 * width] += part
        part = product(lhs_of(rq + q, rows + q), rhs_of(q, width, gates))
        acc[rq * cols : rows * cols, width:gates] += part
        j0 = min(rp + p, rq + q)
        rhs = jnp.concatenate([rhs_of(p, 2 * width, gates), rhs_of(q, 0, width)], axis=1)
        part = product(lhs_of(j0, rows + q), rhs)
        a = (rp + p - j0) * cols
        acc[rp * cols : rows * cols, 2 * width : gates] += part[a : a + (rows - rp) * cols, :width]
        a = (rq + q - j0) * cols
        acc[rq * cols : rows * cols, :width] += part[a : a + (rows - rq) * cols, width:]


def new_state(gates, m_gates, width, c_old, m_old):
    def c_gate(k):
        return gates[:, k * width : (k + 1) * width]

    def m_gate(k):
        return m_gates[:, k * width : (k + 1) * width]

    c_new = sigmoid(c_gate(1) + 1.0) * c_old + sigmoid(c_gate(0)) * jnp.tanh(c_gate(2))
    m_new = sigmoid(m_gate(1) + 1.0) * m_old + sigmoid(m_gate(0)) * jnp.tanh(m_gate(2))
    return c_new, m_new


def pack_kernel(h_hbm, c_hbm, m_hbm, f_hbm, cov_hbm, far, near, c_own, m_own, later, f_ref, cov_ref, sems):
    cols = far.shape[1]
    width = f_ref.shape[2]
    copies = []
    for e in range(4):
        row = own_row(e)
        copies.append((m_hbm.at[row], m_own.at[e]))
        copies.append((c_hbm.at[row], c_own.at[e]))
        copies.append((h_hbm.at[row], far.at[e]))
        if e >= 2:
            copies.append((h_hbm.at[row], near.at[e - 2]))
    copies.append((f_hbm, f_ref))
    copies.append((cov_hbm, cov_ref))
    copies = [pltpu.make_async_copy(a, b, sems.at[i]) for i, (a, b) in enumerate(copies)]
    for copy in copies:
        copy.start()
    for copy in copies:
        copy.wait()
    for e in range(4):
        m = m_own[e].astype(BF)
        far[4 + e] = m
        if e < 2:
            far[8 + e] = c_own[e].astype(BF)
        else:
            near[e] = m
    for unit, moments in enumerate(((0, 1), (2,))):
        parts = []
        for e in range(4):
            row = own_row(e)
            cover = cov_ref[pl.ds(row, 1), :].astype(F32)
            for moment in moments:
                parts.append(f_ref[moment, row].astype(F32) * cover)
        if len(parts) * width < LANES:
            parts.append(jnp.zeros((LANES - len(parts) * width, cols), F32))
        packed = jnp.concatenate(parts, axis=0).T.astype(BF)
        near[4 + unit] = packed
        if unit == 0:
            far[10] = packed
        else:
            later[0] = packed


def memory_kernel(moment, width_in, *refs):
    first = moment == 0
    if first:
        far0, near0, x_hbm, m_hbm, h_hbm, o_hbm, last_hbm, acc, im_x, im, w_x, w_m, w_h, w_o, w_last, pad, sems = refs
        copies = [
            pltpu.make_async_copy(a, b, sems.at[i])
            for i, (a, b) in enumerate(
                ((x_hbm, w_x), (m_hbm, w_m), (h_hbm, w_h), (o_hbm, w_o), (last_hbm, w_last))
            )
        ]
        for copy in copies:
            copy.start()
    else:
        own_x, near0, arrived, m_edge, low_mid, low_in, w_x, w_m, acc, im_x, im, pad = refs
    cols = near0.shape[1]
    width = near0.shape[2]
    clear_pad(pad)
    own_frame = far0[10] if first else own_x[own_x.shape[0] - 1]
    low = 4 if first else 2
    for e in range(4):
        put_row(pad, e, im, e, far0[4 + e] if first else m_edge[e].astype(BF), width, 0)
    for k in range(2):
        if first:
            put_row(pad, 4 + k, im, 4 + k, near0[3 - k], width, 0)
        else:
            put_row(pad, 4 + k, im, 4 + k, low_mid[1, k], width, 0)
            put_row(pad, 6 + k, im, 6 + k, low_in[1, 1 - k], width, 0)
    for e in range(4):
        put_frame(pad, 8 + e, im_x, 4 + e, own_frame, e, moment, width_in)
    for k in range(2):
        put_frame(pad, 12 + k, im_x, 8 + k, near0[4 + moment // 2], 3 - k, moment, width_in)
    if first:
        copies[0].wait()
        copies[1].wait()
    else:
        keep = partner_exists()
        packed = arrived[arrived.shape[0] - 1].astype(F32) * keep
        for k in range(4):
            put_frame(pad, 14 + k, im_x, 3 - k, packed, k, moment, width_in)
    add_memory_pairs(acc, im, im_x, low, 0, w_m, w_x, low, 6)
    if first:
        for copy in copies[2:]:
            copy.wait()


def hidden_kernel(first, *refs):
    hid, hid_in, c_old, m_old, acc_m, im_x, w_x, w_h, acc, low_ref, c_out, m_out, im, pad = refs
    cols = hid.shape[1]
    width = hid.shape[2]
    clear_pad(pad)
    for e in range(4):
        put_row(pad, e, im, e, hid[e], width, 0)
    for k in range(2):
        put_row(pad, 4 + k, im, 4 + k, hid_in[1 - k], width, 0)
    add_taps(acc, None, im, im_x, 4, 0, w_h, w_x, H_PARTS, 4, 10, 6)
    for k in range(2):
        here = slice((4 + k) * cols, (5 + k) * cols)
        old = 2 + k if first else k
        c_new, m_new = new_state(acc[here, :], acc_m[here, :], width, c_old[old], m_old[old])
        c_out[k] = c_new
        m_out[k] = m_new
        low_ref[0, k] = c_new.astype(BF)
        low_ref[1, k] = m_new.astype(BF)


def two_taps(lhs, w_o, p, q):
    rhs = jnp.concatenate([w_o[tap_row(p)], w_o[tap_row(q)]], axis=1)
    return jnp.dot(lhs, rhs, preferred_element_type=F32)


def predict(target, hidden, w_out):
    for e in range(4):
        target[e] = lax.dot_general(
            w_out[...], hidden[e], (((1,), (1,)), ((), ())), preferred_element_type=F32
        ).astype(BF)


def inner_kernel(first, *refs):
    acc_old, acc_m_old, im_h, im_m, im_x, w_x, w_h, w_m, low_mid, w_o = refs[:10]
    if first:
        acc, acc_m, gate, pad, im = refs[10:]
    else:
        hid, w_out, acc, acc_m, gate, predicted, pad, im = refs[10:]
    cols, width = low_mid.shape[2], low_mid.shape[3]
    add_last_tap(acc, im_h, im_x, 4, w_h, w_x, H_PARTS, 4)
    add_last_tap(acc_m, im_m, im_x, 4 if first else 2, w_m, w_x, M_PARTS, 4)
    clear_pad(pad)
    for k in range(2):
        for part in range(2):
            put_row(pad, 2 * k + part, im, k, low_mid[part, k], 2 * width, part * width)
    lhs = im[...].reshape(2 * cols, im.shape[2])
    part = two_taps(lhs, w_o, 4, 3)
    gate[:cols] = part[:cols, :width]
    gate[cols : 2 * cols] = part[cols:, :width] + part[:cols, width:]
    more = two_taps(lhs, w_o, 2, 1)
    gate[2 * cols : 3 * cols] = part[cols:, width:] + more[:cols, :width]
    gate[3 * cols :] = more[cols:, :width] + more[:cols, width:]
    if not first:
        predict(predicted, hid, w_out)


def final_kernel(moment, last, width_in, *refs):
    first = moment == 0
    refs = list(refs)
    if first:
        arrived, c_edge, m_edge, later = refs[:4]
        refs = refs[4:]
    else:
        arrived, c_edge, m_edge, im_x = refs[:4]
        refs = refs[4:]
    acc_in, acc_m_in, low_mid, low_in, gate_in, w_x, w_h, w_m, w_o, w_last = refs[:10]
    refs = refs[10:]
    if last:
        pred1, pred2, c_mid, m_mid, w_out, predicted, c_fin, m_fin = refs[:8]
        refs = refs[8:]
    else:
        far, near, c_out, m_out = refs[:4]
        refs = refs[4:]
    pad, im_h, im_m, im_j, im_i, acc, acc_m, gate = refs[:8]
    if first:
        im_x = refs[8]
    if last:
        keep_c, keep_m, frame, sems = refs[8:]
    cols = arrived.shape[1]
    width = arrived.shape[2]
    m_rows = 4 if first else 2
    clear_pad(pad)
    keep = partner_exists()

    def arrived_row(k):
        return arrived[k].astype(F32) * keep

    for k in range(4):
        put_row(pad, k, im_h, 3 - k, arrived_row(k), width, 0)
    for k in range(m_rows):
        put_row(pad, 4 + k, im_m, 3 - k if first else 1 - k, arrived_row(4 + k), width, 0)
    if first:
        for k in range(4):
            put_frame(pad, 24 + k, im_x, 3 - k, arrived_row(10), k, moment, width_in)
    for k in range(2):
        for part in range(2):
            put_row(pad, 12 + 2 * k + part, im_i, k, low_in[part, 1 - k], 2 * width, part * width)
    add_taps(acc, acc_in, im_h, im_x, 0, 0, w_h, w_x, H_PARTS, 0, 4, 4)
    add_taps(acc_m, acc_m_in, im_m, im_x, 0, 0, w_m, w_x, M_PARTS, 0, m_rows, 4)
    copies = []
    for r in range(4):
        if first and r < 2:
            c_old, m_old = arrived[9 - r].astype(F32), arrived[5 - r].astype(F32)
        elif first:
            c_old, m_old = c_edge[r - 2], m_edge[r - 2]
        else:
            c_old, m_old = c_edge[r], m_edge[r]
        here = slice(r * cols, (r + 1) * cols)
        gates = acc[here, :]
        m_gates = (acc_m if r < m_rows else acc_m_in)[here, :]
        c_new, m_new = new_state(gates, m_gates, width, c_old, m_old)
        if r < 2:
            c_new, m_new = c_new * keep, m_new * keep
        put_row(pad, 16 + 2 * r, im_j, r, c_new.astype(BF), 2 * width, 0)
        put_row(pad, 17 + 2 * r, im_j, r, m_new.astype(BF), 2 * width, width)
        if not last:
            c_out[r] = c_new
            m_out[r] = m_new
        elif r >= 2:
            keep_c[r - 2] = c_new
            keep_m[r - 2] = m_new
    if last:
        for e in range(4):
            sources = (keep_c.at[e], keep_m.at[e]) if e < 2 else (c_mid.at[e - 2], m_mid.at[e - 2])
            for n, (source, target) in enumerate(zip(sources, (c_fin, m_fin))):
                copies.append(pltpu.make_async_copy(source, target.at[own_row(e)], sems.at[2 * e + n]))
            for t, source in enumerate((pred1, pred2)):
                target = predicted.at[t, own_row(e)]
                copies.append(pltpu.make_async_copy(source.at[e], target, sems.at[8 + 2 * e + t]))
        for copy in copies:
            copy.start()
    part = two_taps(im_j[0:4].reshape(4 * cols, -1), w_o, 0, 1)
    gate[...] = part[:, :width] + gate_in[...]
    gate[: 3 * cols] += part[cols:, width:]
    part = two_taps(im_j[2:4].reshape(2 * cols, -1), w_o, 2, 3)
    gate[: 2 * cols] += part[:, :width]
    gate[:cols] += part[cols:, width:]
    part = two_taps(im_i[...].reshape(2 * cols, -1), w_o, 4, 3)
    gate[2 * cols :] += part[:, :width]
    gate[3 * cols :] += part[:cols, width:]
    rows = []
    for e in range(4):
        if e < 2:
            joined = im_j[2 + e, :, REACH * 2 * width : (REACH + 1) * 2 * width]
        else:
            joined = jnp.concatenate([low_mid[0, e - 2], low_mid[1, e - 2]], axis=1)
        mixed = jnp.dot(joined, w_last[...], preferred_element_type=F32)
        source = acc if e < 2 else acc_in
        pre = source[(2 + e) * cols : (3 + e) * cols, 3 * width :]
        pre = pre + gate[e * cols : (e + 1) * cols]
        hidden = (sigmoid(pre) * jnp.tanh(mixed)).astype(BF)
        if last:
            rows.append(hidden)
        else:
            far[e] = hidden
            if e >= 2:
                near[e - 2] = hidden
    if not last:
        for k in range(2):
            far[4 + k] = low_mid[1, k]
        if first:
            far[6] = later[0]
    else:
        for e in range(4):
            frame[e] = lax.dot_general(
                w_out[...], rows[e], (((1,), (1,)), ((), ())), preferred_element_type=F32
            ).astype(BF)
            copies.append(pltpu.make_async_copy(frame.at[e], predicted.at[2, own_row(e)], sems.at[16 + e]))
            copies[-1].start()
        for copy in copies:
            copy.wait()


VMEM = pl.BlockSpec(memory_space=pltpu.VMEM)
HBM = pl.BlockSpec(memory_space=pltpu.HBM)


def call(body, outs, scratch, args, flops, far_args=(), far_outs=(), aliases=None):
    return pl.pallas_call(
        body,
        out_shape=[jax.ShapeDtypeStruct(shape, kind) for shape, kind in outs],
        in_specs=[HBM if i in far_args else VMEM for i in range(len(args))],
        out_specs=[HBM if i in far_outs else VMEM for i in range(len(outs))],
        scratch_shapes=scratch,
        input_output_aliases=aliases or {},
        compiler_params=pltpu.CompilerParams(vmem_limit_bytes=16 * 2**20),
        cost_estimate=pl.CostEstimate(flops=flops, bytes_accessed=4 * 2**20, transcendentals=0),
    )(*args)


def per_device(frames, coverage, h_init, c_init, m_init, w_x, w_h, w_m, w_o, w_last, w_out):
    cols, width = h_init.shape[1], h_init.shape[2]
    width_in = frames.shape[3]
    count = lax.axis_size("row")
    groups = lax.axis_size("groups")
    across = [(g * count + i, g * count + i + 1) for g in range(groups) for i in range(1, count - 1, 2)]
    if groups % 2 == 0:
        across += [(g * count + i, (g + 1) * count + i) for g in range(0, groups, 2) for i in (0, count - 1)]
    across += [(j, i) for i, j in across]
    beside = [(i, i ^ 1) for i in range(count)]
    w_x = w_x.reshape(TAPS, TAPS * width_in, -1)
    w_h = w_h.reshape(TAPS, TAPS * width, -1)
    w_m = w_m.reshape(TAPS, TAPS * width, -1)
    w_o = w_o.reshape(TAPS, TAPS * 2 * width, -1)
    w_out = w_out.T

    def rows(n, kind=BF):
        return ((n, cols, width), kind)

    def shaped(w):
        return (w.shape, w.dtype)

    flat = frames.transpose(0, 1, 3, 2)
    h_init, c_init, m_init, flat, coverage, w_x, w_h, w_m, w_o, w_last = (
        pltpu.with_memory_space_constraint(x, pltpu.HBM)
        for x in (h_init, c_init, m_init, flat, coverage, w_x, w_h, w_m, w_o, w_last)
    )
    far0, near0, c_edge, m_edge, later = call(
        pack_kernel,
        [rows(11), rows(6), rows(4, F32), rows(4, F32), rows(1)],
        [
            pltpu.VMEM(flat.shape, flat.dtype),
            pltpu.VMEM(coverage.shape, coverage.dtype),
            pltpu.SemaphoreType.DMA((16,)),
        ],
        (h_init, c_init, m_init, flat, coverage),
        10**6,
        far_args=range(5),
    )
    near0_in = lax.ppermute(near0, "row", beside)
    arrived = lax.ppermute(far0, ("groups", "row"), across)
    frames_out = []
    for moment in range(STEPS):
        first, last = moment == 0, moment == STEPS - 1
        outs = [
            ((6 * cols, 3 * width), F32),
            ((10, cols, LANES), BF),
            ((6 if first else 8, cols, TAPS * width), BF),
        ]
        scratch = [pltpu.VMEM((18, cols + 16, LANES), F32)]
        if first:
            args = (far0, near0_in, w_x, w_m, w_h, w_o, w_last)
            outs += [shaped(w) for w in args[2:]]
            scratch.append(pltpu.SemaphoreType.DMA((5,)))
            far_args = range(2, 7)
        else:
            args = (later if last else far0, near0_in, frames_in, m_edge, low_mid, low_in, w_x, w_m)
            far_args = ()
        done = call(
            functools.partial(memory_kernel, moment, width_in), outs, scratch, args, 2 * 10**9, far_args
        )
        acc_m, im_x, im_m = done[:3]
        if first:
            w_x, w_m, w_h, w_o, w_last = done[3:]
            args = (far0, near0_in, c_edge, m_edge)
        else:
            args = (far, near_in, c_mid, m_mid)
        outs = [((6 * cols, 4 * width), F32), ((2, 2, cols, width), BF), rows(2, F32), rows(2, F32)]
        outs.append(((6, cols, TAPS * width), BF))
        scratch = [pltpu.VMEM((6, cols + 16, LANES), F32)]
        acc, low_mid, c_mid, m_mid, im_h = call(
            functools.partial(hidden_kernel, first), outs, scratch, args + (acc_m, im_x, w_x, w_h), 2 * 10**9
        )
        low_in = lax.ppermute(low_mid, "row", beside)
        args = (acc, acc_m, im_h, im_m, im_x, w_x, w_h, w_m, low_mid, w_o)
        outs = [((6 * cols, 4 * width), F32), ((6 * cols, 3 * width), F32), ((4 * cols, width), F32)]
        if not first:
            args += (far, w_out)
            outs.append(((4, width_in, cols), BF))
        scratch = [pltpu.VMEM((4, cols + 16, LANES), F32), pltpu.VMEM((2, cols, 2 * TAPS * width), BF)]
        edge = call(functools.partial(inner_kernel, first), outs, scratch, args, 10**9, aliases={0: 0, 1: 1})
        acc, acc_m = edge[:2]
        frames_out += edge[3:]
        frames_in = arrived
        args = (arrived, c_edge, m_edge)
        if first:
            args += (later,)
        if not first:
            args += (im_x,)
        args += (acc, acc_m, low_mid, low_in, edge[2], w_x, w_h, w_m, w_o, w_last)
        far_outs = ()
        if last:
            args += (frames_out[0], frames_out[1], c_mid, m_mid, w_out)
            outs = [((STEPS, 4, width_in, cols), BF), rows(4, F32), rows(4, F32)]
            far_outs = (0, 1, 2)
        else:
            outs = [rows(7 if first else 6), rows(2), rows(4, F32), rows(4, F32)]
        scratch = [
            pltpu.VMEM((32, cols + 16, LANES), F32),
            pltpu.VMEM((4, cols, TAPS * width), BF),
            pltpu.VMEM((4 if first else 2, cols, TAPS * width), BF),
            pltpu.VMEM((4, cols, 2 * TAPS * width), BF),
            pltpu.VMEM((2, cols, 2 * TAPS * width), BF),
            pltpu.VMEM((4 * cols, 4 * width), F32),
            pltpu.VMEM((4 * cols, 3 * width), F32),
            pltpu.VMEM((4 * cols, width), F32),
        ]
        if first:
            scratch.append(pltpu.VMEM((4, cols, LANES), BF))
        if last:
            scratch += [
                pltpu.VMEM(*rows(2, F32)),
                pltpu.VMEM(*rows(2, F32)),
                pltpu.VMEM((4, width_in, cols), BF),
                pltpu.SemaphoreType.DMA((20,)),
            ]
        done = call(
            functools.partial(final_kernel, moment, last, width_in),
            outs, scratch, args, 3 * 10**9, far_outs=far_outs,
        )
        if last:
            predicted, c_final, m_final = done
            return predicted.transpose(0, 1, 3, 2), c_final, m_final
        far, near, c_edge, m_edge = done
        near_in = lax.ppermute(near, "row", beside)
        arrived = lax.ppermute(far, ("groups", "row"), across)


def solution(mesh):
    placed = (
        P("groups", "row", None, None),
        P("row", "groups"),
        P("row", "groups", None),
        P("row", "groups", None),
        P("row", "groups", None),
        P(),
        P(),
        P(),
        P(),
        P(),
        P(),
    )
    return jax.shard_map(
        per_device,
        mesh=mesh,
        in_specs=placed,
        out_specs=(
            P("groups", "row", None, None),
            P("row", "groups", None),
            P("row", "groups", None),
        ),
        check_vma=False,
    )
```

```python
import functools

import jax
import jax.numpy as jnp
from jax import lax
from jax.experimental import pallas as pl
from jax.experimental.pallas import tpu as pltpu
from jax.sharding import PartitionSpec as P

STEPS = 3
TAPS = 5
REACH = 2
LANES = 128
BF = jnp.bfloat16
F32 = jnp.float32


def odd_device():
    return lax.rem(lax.axis_index("row"), 2)


def own_row(e):
    odd = odd_device()
    return e + odd * (3 - 2 * e)


def tap_row(p):
    odd = odd_device()
    return p + odd * (TAPS - 1 - 2 * p)


def partner_exists():
    place = lax.axis_index("row")
    inside = jnp.logical_and(place > 0, place < lax.axis_size("row") - 1)
    return jnp.where(inside, 1.0, 0.0).astype(F32)


def sigmoid(x):
    return 0.5 * jnp.tanh(0.5 * x) + 0.5


def clear_pad(pad):
    rows, height = pad.shape[0], pad.shape[1]
    pad[:, :8] = jnp.zeros((rows, 8, LANES), F32)
    pad[:, height - 8 :] = jnp.zeros((rows, 8, LANES), F32)


def put_row(pad, slot, im, row, value, stride, lane0):
    cols = value.shape[0]
    pad[slot, 8 : 8 + cols] = value.astype(F32)
    for s in range(TAPS):
        im[row, :, s * stride + lane0 : s * stride + lane0 + LANES] = pad[
            slot, 6 + s : 6 + s + cols
        ].astype(BF)


def frame_lane(e, moment, width):
    return width * (2 * e + moment if moment < 2 else e)


def put_frame(pad, slot, im, row, packed, e, moment, width):
    cols = packed.shape[0]
    group = frame_lane(e, moment, width)
    value = packed.astype(F32)
    if group:
        value = pltpu.roll(value, LANES - group, 1)
    lane = lax.broadcasted_iota(jnp.int32, (cols, LANES), 1)
    value = jnp.where(lane < width, value, 0.0)
    pad[slot, 8 : 8 + cols] = value
    total = pad[slot, 6 : 6 + cols]
    for s in range(1, TAPS):
        total = total + pltpu.roll(pad[slot, 6 + s : 6 + s + cols], width * s, 1)
    im[row] = total.astype(BF)


H_PARTS = ((0, 512, ((0, 384), (768, 896))),)
M_PARTS = ((0, 256, ((384, 640),)), (256, 384, ((640, 768),)))


def add_last_tap(acc, im, im_x, row0, weight, w_x, parts, rows):
    cols = im.shape[1]
    p = TAPS - 1
    lhs = jnp.concatenate(
        [
            im[p - row0 : p - row0 + rows].reshape(rows * cols, im.shape[2]),
            im_x[p : p + rows].reshape(rows * cols, LANES),
        ],
        axis=1,
    )
    tap = tap_row(p)
    for c0, c1, x_cols in parts:
        rest = frame_rows(w_x, tap, x_cols)
        rhs = jnp.concatenate([weight[tap, :, c0:c1]] + rest, axis=0)
        acc[: rows * cols, c0:c1] += jnp.dot(lhs, rhs, preferred_element_type=F32)


def add_taps(acc, base, im, im_x, row0, x_row0, weight, w_x, parts, low, high, rows):
    cols = im.shape[1]
    order = range(TAPS) if low == 0 else range(TAPS - 1, -1, -1)
    begun = False
    for p in order:
        r0, r1 = max(0, low - p), min(rows, high - p)
        if low and p == TAPS - 1:
            r0 = TAPS - 1
            acc[: r0 * cols, :] = jnp.zeros((r0 * cols, acc.shape[1]), F32)
        if r0 >= r1:
            continue
        count = (r1 - r0) * cols
        j = r0 + p
        lhs = jnp.concatenate(
            [
                im[j - row0 : j - row0 + r1 - r0].reshape(count, im.shape[2]),
                im_x[j - x_row0 : j - x_row0 + r1 - r0].reshape(count, LANES),
            ],
            axis=1,
        )
        tap = tap_row(p)
        here = slice(r0 * cols, r1 * cols)
        for c0, c1, x_cols in parts:
            frame = jnp.concatenate([w_x[tap, :, x0:x1] for x0, x1 in x_cols], axis=1)
            fill = jnp.zeros((LANES - w_x.shape[1], c1 - c0), BF)
            rhs = jnp.concatenate([weight[tap, :, c0:c1], frame, fill], axis=0)
            part = jnp.dot(lhs, rhs, preferred_element_type=F32)
            if begun:
                acc[here, c0:c1] += part
            elif base is None:
                acc[here, c0:c1] = part
            else:
                acc[here, c0:c1] = base[here, c0:c1] + part
        begun = True


def frame_rows(w_x, tap, spans):
    values = jnp.concatenate([w_x[tap, :, a:b] for a, b in spans], axis=1)
    fill = jnp.zeros((LANES - values.shape[0], values.shape[1]), BF)
    return [values, fill]


def add_memory_pairs(acc, im, im_x, row0, x_row0, weight, w_x, low, rows):
    cols = im.shape[1]
    width = weight.shape[2] // 3
    gates = 3 * width

    def lhs_of(j0, j1):
        count = (j1 - j0) * cols
        return jnp.concatenate(
            [
                im[j0 - row0 : j1 - row0].reshape(count, im.shape[2]),
                im_x[j0 - x_row0 : j1 - x_row0].reshape(count, LANES),
            ],
            axis=1,
        )

    def rhs_of(p, a, b):
        tap = tap_row(p)
        rest = frame_rows(w_x, tap, ((gates + a, gates + b),))
        return jnp.concatenate([weight[tap, :, a:b]] + rest, axis=0)

    def product(lhs, rhs):
        return jnp.dot(lhs, rhs, preferred_element_type=F32)

    p = TAPS - 1
    r0 = 4
    acc[: r0 * cols, :] = jnp.zeros((r0 * cols, gates), F32)
    lhs = lhs_of(r0 + p, rows + p)
    for a, b in ((0, 2 * width), (2 * width, gates)):
        acc[r0 * cols : rows * cols, a:b] = product(lhs, rhs_of(p, a, b))
    for p in (2, 0):
        q = p + 1
        rp, rq = max(0, low - p), max(0, low - q)
        part = product(lhs_of(rp + p, rows + p), rhs_of(p, 0, 2 * width))
        acc[rp * cols : rows * cols, : 2 * width] += part
        part = product(lhs_of(rq + q, rows + q), rhs_of(q, width, gates))
        acc[rq * cols : rows * cols, width:gates] += part
        j0 = min(rp + p, rq + q)
        rhs = jnp.concatenate([rhs_of(p, 2 * width, gates), rhs_of(q, 0, width)], axis=1)
        part = product(lhs_of(j0, rows + q), rhs)
        a = (rp + p - j0) * cols
        acc[rp * cols : rows * cols, 2 * width : gates] += part[a : a + (rows - rp) * cols, :width]
        a = (rq + q - j0) * cols
        acc[rq * cols : rows * cols, :width] += part[a : a + (rows - rq) * cols, width:]


def new_state(gates, m_gates, width, c_old, m_old):
    def c_gate(k):
        return gates[:, k * width : (k + 1) * width]

    def m_gate(k):
        return m_gates[:, k * width : (k + 1) * width]

    c_new = sigmoid(c_gate(1) + 1.0) * c_old + sigmoid(c_gate(0)) * jnp.tanh(c_gate(2))
    m_new = sigmoid(m_gate(1) + 1.0) * m_old + sigmoid(m_gate(0)) * jnp.tanh(m_gate(2))
    return c_new, m_new


def pack_kernel(h_hbm, c_hbm, m_hbm, f_hbm, cov_hbm, far, near, c_own, m_own, later, f_ref, cov_ref, sems):
    cols = far.shape[1]
    width = f_ref.shape[2]
    copies = []
    for e in range(4):
        row = own_row(e)
        copies.append((m_hbm.at[row], m_own.at[e]))
        copies.append((c_hbm.at[row], c_own.at[e]))
        copies.append((h_hbm.at[row], far.at[e]))
        if e >= 2:
            copies.append((h_hbm.at[row], near.at[e - 2]))
    copies.append((f_hbm, f_ref))
    copies.append((cov_hbm, cov_ref))
    copies = [pltpu.make_async_copy(a, b, sems.at[i]) for i, (a, b) in enumerate(copies)]
    for copy in copies:
        copy.start()
    for copy in copies:
        copy.wait()
    for e in range(4):
        m = m_own[e].astype(BF)
        far[4 + e] = m
        if e < 2:
            far[8 + e] = c_own[e].astype(BF)
        else:
            near[e] = m
    for unit, moments in enumerate(((0, 1), (2,))):
        parts = []
        for e in range(4):
            row = own_row(e)
            cover = cov_ref[pl.ds(row, 1), :].astype(F32)
            for moment in moments:
                parts.append(f_ref[moment, row].astype(F32) * cover)
        if len(parts) * width < LANES:
            parts.append(jnp.zeros((LANES - len(parts) * width, cols), F32))
        packed = jnp.concatenate(parts, axis=0).T.astype(BF)
        near[4 + unit] = packed
        if unit == 0:
            far[10] = packed
        else:
            later[0] = packed


def memory_kernel(moment, width_in, *refs):
    first = moment == 0
    if first:
        far0, near0, x_hbm, m_hbm, h_hbm, o_hbm, last_hbm, acc, im_x, im, w_x, w_m, w_h, w_o, w_last, pad, sems = refs
        copies = [
            pltpu.make_async_copy(a, b, sems.at[i])
            for i, (a, b) in enumerate(
                ((x_hbm, w_x), (m_hbm, w_m), (h_hbm, w_h), (o_hbm, w_o), (last_hbm, w_last))
            )
        ]
        for copy in copies:
            copy.start()
    else:
        own_x, near0, arrived, m_edge, low_mid, low_in, w_x, w_m, acc, im_x, im, pad = refs
    cols = near0.shape[1]
    width = near0.shape[2]
    clear_pad(pad)
    own_frame = far0[10] if first else own_x[own_x.shape[0] - 1]
    low = 4 if first else 2
    for e in range(4):
        put_row(pad, e, im, e, far0[4 + e] if first else m_edge[e].astype(BF), width, 0)
    for k in range(2):
        if first:
            put_row(pad, 4 + k, im, 4 + k, near0[3 - k], width, 0)
        else:
            put_row(pad, 4 + k, im, 4 + k, low_mid[1, k], width, 0)
            put_row(pad, 6 + k, im, 6 + k, low_in[1, 1 - k], width, 0)
    for e in range(4):
        put_frame(pad, 8 + e, im_x, 4 + e, own_frame, e, moment, width_in)
    for k in range(2):
        put_frame(pad, 12 + k, im_x, 8 + k, near0[4 + moment // 2], 3 - k, moment, width_in)
    if first:
        copies[0].wait()
        copies[1].wait()
    else:
        keep = partner_exists()
        packed = arrived[arrived.shape[0] - 1].astype(F32) * keep
        for k in range(4):
            put_frame(pad, 14 + k, im_x, 3 - k, packed, k, moment, width_in)
    add_memory_pairs(acc, im, im_x, low, 0, w_m, w_x, low, 6)
    if first:
        for copy in copies[2:]:
            copy.wait()


def hidden_kernel(first, *refs):
    hid, hid_in, c_old, m_old, acc_m, im_x, w_x, w_h, acc, low_ref, c_out, m_out, im, pad = refs
    cols = hid.shape[1]
    width = hid.shape[2]
    clear_pad(pad)
    for e in range(4):
        put_row(pad, e, im, e, hid[e], width, 0)
    for k in range(2):
        put_row(pad, 4 + k, im, 4 + k, hid_in[1 - k], width, 0)
    add_taps(acc, None, im, im_x, 4, 0, w_h, w_x, H_PARTS, 4, 10, 6)
    for k in range(2):
        here = slice((4 + k) * cols, (5 + k) * cols)
        old = 2 + k if first else k
        c_new, m_new = new_state(acc[here, :], acc_m[here, :], width, c_old[old], m_old[old])
        c_out[k] = c_new
        m_out[k] = m_new
        low_ref[0, k] = c_new.astype(BF)
        low_ref[1, k] = m_new.astype(BF)


def two_taps(lhs, w_o, p, q):
    rhs = jnp.concatenate([w_o[tap_row(p)], w_o[tap_row(q)]], axis=1)
    return jnp.dot(lhs, rhs, preferred_element_type=F32)


def predict(target, hidden, w_out):
    for e in range(4):
        target[e] = lax.dot_general(
            w_out[...], hidden[e], (((1,), (1,)), ((), ())), preferred_element_type=F32
        ).astype(BF)


def inner_kernel(first, *refs):
    acc_old, acc_m_old, im_h, im_m, im_x, w_x, w_h, w_m, low_mid, w_o = refs[:10]
    if first:
        acc, acc_m, gate, pad, im = refs[10:]
    else:
        hid, w_out, acc, acc_m, gate, predicted, pad, im = refs[10:]
    cols, width = low_mid.shape[2], low_mid.shape[3]
    add_last_tap(acc, im_h, im_x, 4, w_h, w_x, H_PARTS, 4)
    add_last_tap(acc_m, im_m, im_x, 4 if first else 2, w_m, w_x, M_PARTS, 4)
    clear_pad(pad)
    for k in range(2):
        for part in range(2):
            put_row(pad, 2 * k + part, im, k, low_mid[part, k], 2 * width, part * width)
    lhs = im[...].reshape(2 * cols, im.shape[2])
    part = two_taps(lhs, w_o, 4, 3)
    gate[:cols] = part[:cols, :width]
    gate[cols : 2 * cols] = part[cols:, :width] + part[:cols, width:]
    more = two_taps(lhs, w_o, 2, 1)
    gate[2 * cols : 3 * cols] = part[cols:, width:] + more[:cols, :width]
    gate[3 * cols :] = more[cols:, :width] + more[:cols, width:]
    if not first:
        predict(predicted, hid, w_out)


def final_kernel(moment, last, width_in, *refs):
    first = moment == 0
    refs = list(refs)
    if first:
        arrived, c_edge, m_edge, later = refs[:4]
        refs = refs[4:]
    else:
        arrived, c_edge, m_edge, im_x = refs[:4]
        refs = refs[4:]
    acc_in, acc_m_in, low_mid, low_in, gate_in, w_x, w_h, w_m, w_o, w_last = refs[:10]
    refs = refs[10:]
    if last:
        pred1, pred2, c_mid, m_mid, w_out, predicted, c_fin, m_fin = refs[:8]
        refs = refs[8:]
    else:
        far, near, c_out, m_out = refs[:4]
        refs = refs[4:]
    pad, im_h, im_m, im_j, im_i, acc, acc_m, gate = refs[:8]
    if first:
        im_x = refs[8]
    if last:
        keep_c, keep_m, frame, sems = refs[8:]
    cols = arrived.shape[1]
    width = arrived.shape[2]
    m_rows = 4 if first else 2
    clear_pad(pad)
    keep = partner_exists()

    def arrived_row(k):
        return arrived[k].astype(F32) * keep

    for k in range(4):
        put_row(pad, k, im_h, 3 - k, arrived_row(k), width, 0)
    for k in range(m_rows):
        put_row(pad, 4 + k, im_m, 3 - k if first else 1 - k, arrived_row(4 + k), width, 0)
    if first:
        for k in range(4):
            put_frame(pad, 24 + k, im_x, 3 - k, arrived_row(10), k, moment, width_in)
    for k in range(2):
        for part in range(2):
            put_row(pad, 12 + 2 * k + part, im_i, k, low_in[part, 1 - k], 2 * width, part * width)
    add_taps(acc, acc_in, im_h, im_x, 0, 0, w_h, w_x, H_PARTS, 0, 4, 4)
    add_taps(acc_m, acc_m_in, im_m, im_x, 0, 0, w_m, w_x, M_PARTS, 0, m_rows, 4)
    copies = []
    for r in range(4):
        if first and r < 2:
            c_old, m_old = arrived[9 - r].astype(F32), arrived[5 - r].astype(F32)
        elif first:
            c_old, m_old = c_edge[r - 2], m_edge[r - 2]
        else:
            c_old, m_old = c_edge[r], m_edge[r]
        here = slice(r * cols, (r + 1) * cols)
        gates = acc[here, :]
        m_gates = (acc_m if r < m_rows else acc_m_in)[here, :]
        c_new, m_new = new_state(gates, m_gates, width, c_old, m_old)
        if r < 2:
            c_new, m_new = c_new * keep, m_new * keep
        put_row(pad, 16 + 2 * r, im_j, r, c_new.astype(BF), 2 * width, 0)
        put_row(pad, 17 + 2 * r, im_j, r, m_new.astype(BF), 2 * width, width)
        if not last:
            c_out[r] = c_new
            m_out[r] = m_new
        elif r >= 2:
            keep_c[r - 2] = c_new
            keep_m[r - 2] = m_new
    if last:
        for e in range(4):
            sources = (keep_c.at[e], keep_m.at[e]) if e < 2 else (c_mid.at[e - 2], m_mid.at[e - 2])
            for n, (source, target) in enumerate(zip(sources, (c_fin, m_fin))):
                copies.append(pltpu.make_async_copy(source, target.at[own_row(e)], sems.at[2 * e + n]))
            for t, source in enumerate((pred1, pred2)):
                target = predicted.at[t, own_row(e)]
                copies.append(pltpu.make_async_copy(source.at[e], target, sems.at[8 + 2 * e + t]))
        for copy in copies:
            copy.start()
    part = two_taps(im_j[0:4].reshape(4 * cols, -1), w_o, 0, 1)
    gate[...] = part[:, :width] + gate_in[...]
    gate[: 3 * cols] += part[cols:, width:]
    part = two_taps(im_j[2:4].reshape(2 * cols, -1), w_o, 2, 3)
    gate[: 2 * cols] += part[:, :width]
    gate[:cols] += part[cols:, width:]
    part = two_taps(im_i[...].reshape(2 * cols, -1), w_o, 4, 3)
    gate[2 * cols :] += part[:, :width]
    gate[3 * cols :] += part[:cols, width:]
    rows = []
    for e in range(4):
        if e < 2:
            joined = im_j[2 + e, :, REACH * 2 * width : (REACH + 1) * 2 * width]
        else:
            joined = jnp.concatenate([low_mid[0, e - 2], low_mid[1, e - 2]], axis=1)
        mixed = jnp.dot(joined, w_last[...], preferred_element_type=F32)
        source = acc if e < 2 else acc_in
        pre = source[(2 + e) * cols : (3 + e) * cols, 3 * width :]
        pre = pre + gate[e * cols : (e + 1) * cols]
        hidden = (sigmoid(pre) * jnp.tanh(mixed)).astype(BF)
        if last:
            rows.append(hidden)
        else:
            far[e] = hidden
            if e >= 2:
                near[e - 2] = hidden
    if not last:
        for k in range(2):
            far[4 + k] = low_mid[1, k]
        if first:
            far[6] = later[0]
    else:
        for e in range(4):
            frame[e] = lax.dot_general(
                w_out[...], rows[e], (((1,), (1,)), ((), ())), preferred_element_type=F32
            ).astype(BF)
            copies.append(pltpu.make_async_copy(frame.at[e], predicted.at[2, own_row(e)], sems.at[16 + e]))
            copies[-1].start()
        for copy in copies:
            copy.wait()


VMEM = pl.BlockSpec(memory_space=pltpu.VMEM)
HBM = pl.BlockSpec(memory_space=pltpu.HBM)


def call(body, outs, scratch, args, flops, far_args=(), far_outs=(), aliases=None):
    return pl.pallas_call(
        body,
        out_shape=[jax.ShapeDtypeStruct(shape, kind) for shape, kind in outs],
        in_specs=[HBM if i in far_args else VMEM for i in range(len(args))],
        out_specs=[HBM if i in far_outs else VMEM for i in range(len(outs))],
        scratch_shapes=scratch,
        input_output_aliases=aliases or {},
        compiler_params=pltpu.CompilerParams(vmem_limit_bytes=16 * 2**20),
        cost_estimate=pl.CostEstimate(flops=flops, bytes_accessed=4 * 2**20, transcendentals=0),
    )(*args)


def per_device(frames, coverage, h_init, c_init, m_init, w_x, w_h, w_m, w_o, w_last, w_out):
    cols, width = h_init.shape[1], h_init.shape[2]
    width_in = frames.shape[3]
    count = lax.axis_size("row")
    groups = lax.axis_size("groups")
    across = [(g * count + i, g * count + i + 1) for g in range(groups) for i in range(1, count - 1, 2)]
    if groups % 2 == 0:
        across += [(g * count + i, (g + 1) * count + i) for g in range(0, groups, 2) for i in (0, count - 1)]
    across += [(j, i) for i, j in across]
    beside = [(i, i ^ 1) for i in range(count)]
    w_x = w_x.reshape(TAPS, TAPS * width_in, -1)
    w_h = w_h.reshape(TAPS, TAPS * width, -1)
    w_m = w_m.reshape(TAPS, TAPS * width, -1)
    w_o = w_o.reshape(TAPS, TAPS * 2 * width, -1)
    w_out = w_out.T

    def rows(n, kind=BF):
        return ((n, cols, width), kind)

    def shaped(w):
        return (w.shape, w.dtype)

    flat = frames.transpose(0, 1, 3, 2)
    h_init, c_init, m_init, flat, coverage, w_x, w_h, w_m, w_o, w_last = (
        pltpu.with_memory_space_constraint(x, pltpu.HBM)
        for x in (h_init, c_init, m_init, flat, coverage, w_x, w_h, w_m, w_o, w_last)
    )
    far0, near0, c_edge, m_edge, later = call(
        pack_kernel,
        [rows(11), rows(6), rows(4, F32), rows(4, F32), rows(1)],
        [
            pltpu.VMEM(flat.shape, flat.dtype),
            pltpu.VMEM(coverage.shape, coverage.dtype),
            pltpu.SemaphoreType.DMA((16,)),
        ],
        (h_init, c_init, m_init, flat, coverage),
        10**6,
        far_args=range(5),
    )
    near0_in = lax.ppermute(near0, "row", beside)
    arrived = lax.ppermute(far0, ("groups", "row"), across)
    frames_out = []
    for moment in range(STEPS):
        first, last = moment == 0, moment == STEPS - 1
        outs = [
            ((6 * cols, 3 * width), F32),
            ((10, cols, LANES), BF),
            ((6 if first else 8, cols, TAPS * width), BF),
        ]
        scratch = [pltpu.VMEM((18, cols + 16, LANES), F32)]
        if first:
            args = (far0, near0_in, w_x, w_m, w_h, w_o, w_last)
            outs += [shaped(w) for w in args[2:]]
            scratch.append(pltpu.SemaphoreType.DMA((5,)))
            far_args = range(2, 7)
        else:
            args = (later if last else far0, near0_in, frames_in, m_edge, low_mid, low_in, w_x, w_m)
            far_args = ()
        done = call(
            functools.partial(memory_kernel, moment, width_in), outs, scratch, args, 2 * 10**9, far_args
        )
        acc_m, im_x, im_m = done[:3]
        if first:
            w_x, w_m, w_h, w_o, w_last = done[3:]
            args = (far0, near0_in, c_edge, m_edge)
        else:
            args = (far, near_in, c_mid, m_mid)
        outs = [((6 * cols, 4 * width), F32), ((2, 2, cols, width), BF), rows(2, F32), rows(2, F32)]
        outs.append(((6, cols, TAPS * width), BF))
        scratch = [pltpu.VMEM((6, cols + 16, LANES), F32)]
        acc, low_mid, c_mid, m_mid, im_h = call(
            functools.partial(hidden_kernel, first), outs, scratch, args + (acc_m, im_x, w_x, w_h), 2 * 10**9
        )
        low_in = lax.ppermute(low_mid, "row", beside)
        args = (acc, acc_m, im_h, im_m, im_x, w_x, w_h, w_m, low_mid, w_o)
        outs = [((6 * cols, 4 * width), F32), ((6 * cols, 3 * width), F32), ((4 * cols, width), F32)]
        if not first:
            args += (far, w_out)
            outs.append(((4, width_in, cols), BF))
        scratch = [pltpu.VMEM((4, cols + 16, LANES), F32), pltpu.VMEM((2, cols, 2 * TAPS * width), BF)]
        edge = call(functools.partial(inner_kernel, first), outs, scratch, args, 10**9, aliases={0: 0, 1: 1})
        acc, acc_m = edge[:2]
        frames_out += edge[3:]
        frames_in = arrived
        args = (arrived, c_edge, m_edge)
        if first:
            args += (later,)
        if not first:
            args += (im_x,)
        args += (acc, acc_m, low_mid, low_in, edge[2], w_x, w_h, w_m, w_o, w_last)
        far_outs = ()
        if last:
            args += (frames_out[0], frames_out[1], c_mid, m_mid, w_out)
            outs = [((STEPS, 4, width_in, cols), BF), rows(4, F32), rows(4, F32)]
            far_outs = (0, 1, 2)
        else:
            outs = [rows(7 if first else 6), rows(2), rows(4, F32), rows(4, F32)]
        scratch = [
            pltpu.VMEM((32, cols + 16, LANES), F32),
            pltpu.VMEM((4, cols, TAPS * width), BF),
            pltpu.VMEM((4 if first else 2, cols, TAPS * width), BF),
            pltpu.VMEM((4, cols, 2 * TAPS * width), BF),
            pltpu.VMEM((2, cols, 2 * TAPS * width), BF),
            pltpu.VMEM((4 * cols, 4 * width), F32),
            pltpu.VMEM((4 * cols, 3 * width), F32),
            pltpu.VMEM((4 * cols, width), F32),
        ]
        if first:
            scratch.append(pltpu.VMEM((4, cols, LANES), BF))
        if last:
            scratch += [
                pltpu.VMEM(*rows(2, F32)),
                pltpu.VMEM(*rows(2, F32)),
                pltpu.VMEM((4, width_in, cols), BF),
                pltpu.SemaphoreType.DMA((20,)),
            ]
        done = call(
            functools.partial(final_kernel, moment, last, width_in),
            outs, scratch, args, 3 * 10**9, far_outs=far_outs,
        )
        if last:
            predicted, c_final, m_final = done
            return predicted.transpose(0, 1, 3, 2), c_final, m_final
        far, near, c_edge, m_edge = done
        near_in = lax.ppermute(near, "row", beside)
        arrived = lax.ppermute(far, ("groups", "row"), across)


def solution(mesh):
    placed = (
        P("groups", "row", None, None),
        P("row", "groups"),
        P("row", "groups", None),
        P("row", "groups", None),
        P("row", "groups", None),
        P(),
        P(),
        P(),
        P(),
        P(),
        P(),
    )
    return jax.shard_map(
        per_device,
        mesh=mesh,
        in_specs=placed,
        out_specs=(
            P("groups", "row", None, None),
            P("row", "groups", None),
            P("row", "groups", None),
        ),
        check_vma=False,
    )
```
